256 devices in a mesh: coal: 8 (over z_lo, core), section: 4 (over y), tensor: 8 (over x, z_hi).
Axes of the slice: x: 4, y: 4, z: 8 (z_hi: 2, z_lo: 4; z = z_hi * 4 + z_lo), core: 2. Of those that a mesh axis runs over, the one named last changes fastest.
Arguments:
- hidden: bfloat16 [32, 128, 8192], P('coal', None, 'section'), parts along dimension 0, may hold values from -120 to 120
- norm_gain: float32 [8192], P('section'), may hold values from 0.1 to 1.9
- w_query: bfloat16 [8192, 8192], P('section', 'tensor'), may hold values from -0.0625 to 0.0625
- w_key: bfloat16 [8192, 1024], P('section', 'tensor'), may hold values from -0.0625 to 0.0625
- w_value: bfloat16 [8192, 1024], P('section', 'tensor'), may hold values from -0.0625 to 0.0625
- w_out: bfloat16 [8192, 8192], P('tensor', 'section'), may hold values from -0.0625 to 0.0625
- cache_key: bfloat16 [8192, 1024], P('section', 'tensor'), may hold values from -400 to 400
- cache_value: bfloat16 [8192, 1024], P('section', 'tensor'), may hold values from -6 to 6
- block_mask: int32 [32, 128], P('coal'), parts along dimension 0, may hold values from 0 to 1
Outputs:
- attn_out: bfloat16 [32, 128, 8192], P('coal', None, ('section', 'tensor')), parts along dimension 0
The draws below stay inside these ranges and needn't reach their ends.
There are 8 independent parts, one for each index of `coal`. The reference program is written for one: setup_inputs(seed, part) draws one part's arguments, and reference() takes and returns one part's arrays. A program takes and returns all parts, laid end to end along the dimension named above; an argument that names none is the same for every part. Nothing has to cross between parts.
All inputs are finite; a program needn't handle non-finite values.
Results may differ from the reference program's by a relative error of at most 0.015.
Values may be sent and summed in bfloat16 or wider, within the bound.
No kernel may reach another device: no remote copies, remote signals or barrier semaphores. Data moves between devices by JAX's collectives and lax.ppermute only.
A program may use at most 128 MiB of HBM per device.

```python
import math
import jax
import jax.numpy as jnp
from jax import lax

D = 8192
HEADS = 64
KVH = 8
HD = 128
NBLK = 128
BLOCK = 64
COAL = 4
ANS = 128


def draw_hidden(key, part):
    key = jax.random.fold_in(key, 11)
    jitter = jax.random.uniform(jax.random.fold_in(key, 1), (D,), jnp.float32)
    column_scale = jnp.exp(math.log(10.0) * (jnp.arange(D).astype(jnp.float32) + jitter) / D)
    base = jnp.clip(jax.random.normal(jax.random.fold_in(key, 2), (COAL, ANS, D), jnp.float32), -6.0, 6.0)
    return (base * column_scale).astype(jnp.bfloat16)


def draw_cache_key(key, part):
    key = jax.random.fold_in(key, 23)
    context = NBLK * BLOCK
    base = jnp.clip(jax.random.normal(jax.random.fold_in(key, 1), (context, KVH * HD), jnp.float32), -6.0, 6.0)
    return base.astype(jnp.bfloat16)


def draw_block_mask(key, part):
    key = jax.random.fold_in(key, 37)
    keep_rate = jax.random.randint(jax.random.fold_in(key, 1), (COAL, 1), 1, 4)
    rolled = jax.random.randint(jax.random.fold_in(key, 2), (COAL, NBLK), 0, 4)
    return (rolled < keep_rate).astype(jnp.int32)


def levels(key, dims, shards, least, high):
    def one(axis_at, blocks):
        steps = jax.random.uniform(jax.random.fold_in(jax.random.fold_in(key, 6), axis_at), (blocks,), jnp.float32, least / len(shards), high / len(shards))
        return jnp.repeat(jnp.exp(steps), dims[axis_at] // blocks).reshape((-1,) + (1,) * (len(dims) - axis_at - 1))

    gain = one(*shards[0])
    for cut in shards[1:]:
        gain = gain * one(*cut)
    return gain


def gaussian(key, shape, scale, bound, cuts=(), dtype=jnp.bfloat16):
    result = jax.random.normal(key, shape, jnp.float32) * scale
    if len(cuts) > 0:
        result = levels(key, shape, cuts, -0.22, 0.18) * result
    return jnp.clip(result, min=-bound, max=bound).astype(dtype)


def setup_inputs(seed: int = 0, part: int = 0) -> dict:
    keys = jax.random.split(jax.random.key(seed), 10)
    part_splits = jax.random.split(jax.random.fold_in(keys[9], part), 10)
    return {
        "hidden": draw_hidden(jax.random.fold_in(jax.random.fold_in(keys[9], part), 71), part),
        "norm_gain": jnp.clip(1.0 + 0.18 * jax.random.normal(keys[1], (D,), jnp.float32), 0.1, 1.9),
        "w_query": gaussian(keys[2], (D, HEADS * HD), D ** -0.5, 0.0625, ((0, 4), (1, 8))),
        "w_key": gaussian(keys[3], (D, KVH * HD), D ** -0.5, 0.0625, ((0, 4), (1, 8))),
        "w_value": gaussian(keys[4], (D, KVH * HD), D ** -0.5, 0.0625, ((0, 4), (1, 8))),
        "w_out": gaussian(keys[5], (HEADS * HD, D), (HEADS * HD) ** -0.5, 0.0625, ((0, 8), (1, 4))),
        "cache_key": draw_cache_key(jax.random.fold_in(keys[9], 71), part),
        "cache_value": gaussian(keys[7], (NBLK * BLOCK, KVH * HD), 1.0, 6.0, ((0, 4), (1, 8))),
        "block_mask": draw_block_mask(jax.random.fold_in(jax.random.fold_in(keys[9], part), 71), part),
    }


rope_base = 500000.0
norm_eps = 1e-05
masked_score = -1e+30

def rotate(tensor, positions):
    half_dim = tensor.shape[-1] // 2
    frequency = rope_base ** (-2.0 * jnp.arange(half_dim).astype(jnp.float32) / tensor.shape[-1])
    angles = positions[:, None] * frequency[None, :]
    cosine = jnp.cos(angles)[:, None, :]
    sine_part = jnp.sin(angles)[:, None, :]
    first_half = tensor[..., :half_dim]
    second = tensor[..., half_dim:]
    return jnp.concatenate([first_half * cosine - second * sine_part, second * cosine + first_half * sine_part], axis=-1)

def reference(hidden, norm_gain, w_query, w_key, w_value, w_out, cache_key, cache_value, block_mask):
    context = NBLK * BLOCK
    group_size = HEADS // KVH
    hidden_f32 = hidden.astype(jnp.float32)
    mean_square = lax.optimization_barrier(jnp.mean(hidden_f32 * hidden_f32, axis=-1, keepdims=True))
    normed = (hidden_f32 * lax.rsqrt(mean_square + norm_eps) * norm_gain).astype(jnp.bfloat16).reshape(COAL * ANS, D)
    queries = jnp.dot(normed, w_query, preferred_element_type=jnp.float32).reshape(COAL, ANS, HEADS, HD)
    new_keys = jnp.dot(normed, w_key, preferred_element_type=jnp.float32).reshape(COAL, ANS, KVH, HD)
    new_values = jnp.dot(normed, w_value, preferred_element_type=jnp.float32).reshape(COAL, ANS, KVH, HD)
    positions = (context + jnp.arange(ANS)).astype(jnp.float32)
    queries = rotate(queries, positions).astype(jnp.bfloat16).reshape(COAL, ANS, KVH, group_size, HD)
    new_keys = rotate(new_keys, positions).astype(jnp.bfloat16)
    new_values = new_values.astype(jnp.bfloat16)
    cache_keys = cache_key.reshape(context, KVH, HD).astype(jnp.float32)
    cache_values = cache_value.reshape(context, KVH, HD).astype(jnp.float32)
    kept_blocks = jnp.broadcast_to((block_mask > 0)[:, :, None], (COAL, NBLK, BLOCK)).reshape(COAL, context)
    causal = jnp.arange(ANS)[:, None] >= jnp.arange(ANS)[None, :]
    score_scale = 1.0 / math.sqrt(HD)

    def one_coalition(inputs):
        query_block, block_key_rows, block_value_rows, kept_row = inputs
        query_float32 = query_block.astype(jnp.float32)
        far_scores = jnp.einsum('akgd,pkd->kgap', query_float32, cache_keys) * score_scale
        far_scores = jnp.where(kept_row[None, None, None, :], far_scores, masked_score)
        nearby_scores = jnp.einsum('ovxq,wvq->vxow', query_float32, block_key_rows.astype(jnp.float32)) * score_scale
        nearby_scores = jnp.where(causal[None, None], nearby_scores, masked_score)
        maxima = jnp.maximum(lax.optimization_barrier(jnp.max(far_scores, axis=-1)), lax.optimization_barrier(jnp.max(nearby_scores, axis=-1)))[..., None]
        far_weights = jnp.exp(far_scores - maxima)
        near_weights = jnp.exp(nearby_scores - maxima)
        totals = lax.optimization_barrier(jnp.sum(far_weights, axis=-1)) + lax.optimization_barrier(jnp.sum(near_weights, axis=-1))
        far_round = lax.optimization_barrier(far_weights.astype(jnp.bfloat16)).astype(jnp.float32)
        nearby_rounded = lax.optimization_barrier(near_weights.astype(jnp.bfloat16)).astype(jnp.float32)
        weighted_values = jnp.einsum('kgap,pkd->akgd', far_round, cache_values)
        weighted_values = weighted_values + jnp.einsum('rsij,jrz->irsz', nearby_rounded, block_value_rows.astype(jnp.float32))
        attended = weighted_values / jnp.transpose(totals, (2, 0, 1))[..., None]
        return attended.reshape(ANS, HEADS * HD).astype(jnp.bfloat16)
    attention = lax.map(one_coalition, (queries, new_keys, new_values, kept_blocks))
    output = jnp.dot(attention.reshape(COAL * ANS, HEADS * HD), w_out, preferred_element_type=jnp.float32)
    return output.astype(jnp.bfloat16).reshape(COAL, ANS, D)
```

```python
import math

import jax
import jax.numpy as jnp
from jax import lax
from jax.experimental import pallas as pl
from jax.experimental.pallas import tpu as pltpu
from jax.sharding import PartitionSpec as P

D = 8192
HD = 128
NBLK = 128
BLOCK = 64
rope_base = 500000.0
norm_eps = 1e-05
masked_score = -1e30
BF = jnp.bfloat16
F32 = jnp.float32
VMEM_LIMIT = 60 * 1024 * 1024


def section_shift(x, by):
    n = lax.axis_size("section")
    return lax.ppermute(x, "section", [(i, (i + by) % n) for i in range(n)])


def x_shift(x, by):
    n = lax.axis_size("tensor") // 2
    return lax.ppermute(
        x, "tensor", [(i, ((i // 2 + by) % n) * 2 + i % 2) for i in range(2 * n)]
    )


def z_swap(x):
    return lax.ppermute(x, "tensor", [(i, i ^ 1) for i in range(lax.axis_size("tensor"))])


def core_swap(x):
    return lax.ppermute(x, "coal", [(i, i ^ 1) for i in range(lax.axis_size("coal"))])


def project_kernel(place, hidden, gain, w_query, w_key, w_value, o0, o1, o2, o3, scaled):
    outs = (o0, o1, o2, o3)
    step = pl.program_id(0)
    count, answer, _ = hidden.shape
    last = pl.num_programs(0) - 1

    @pl.when(step == 0)
    def _():
        lane = lax.broadcasted_iota(jnp.int32, (answer, 128), 1)
        for r in range(count):
            c = lax.rem(place[0] + r, count)
            rows = hidden[c].astype(F32)
            total = jnp.sum(rows * rows, axis=-1, keepdims=True)
            high = total.astype(BF).astype(F32)
            low = total - high
            outs[r][:, 1280:] = jnp.where(
                lane == 0, high, jnp.where(lane == 1, low, 0.0)
            ).astype(BF)
            scaled[r * answer : (r + 1) * answer] = (rows * gain[...]).astype(BF)

    @pl.when(step < last)
    def _():
        product = jnp.dot(scaled[...], w_query[...], preferred_element_type=F32)
        for r in range(count):
            outs[r][:, pl.ds(pl.multiple_of(step * 256, 256), 256)] = product[
                r * answer : (r + 1) * answer
            ].astype(BF)

    @pl.when(step == last)
    def _():
        weights = jnp.concatenate([w_key[...], w_value[...]], axis=1)
        product = jnp.dot(scaled[...], weights, preferred_element_type=F32)
        for r in range(count):
            outs[r][:, 1024:1280] = product[r * answer : (r + 1) * answer].astype(BF)


def project(place, hidden, gain, w_query, w_key, w_value):
    count, answer, width = hidden.shape
    steps = w_query.shape[1] // 256
    out = jax.ShapeDtypeStruct((answer, 1408), BF)
    whole = lambda *shape: pl.BlockSpec(shape, lambda i, place: (0,) * len(shape))
    return pl.pallas_call(
        project_kernel,
        grid_spec=pltpu.PrefetchScalarGridSpec(
            num_scalar_prefetch=1,
            grid=(steps + 1,),
            in_specs=[
                whole(count, answer, width),
                whole(1, width),
                pl.BlockSpec((width, 256), lambda i, place: (0, jnp.minimum(i, steps - 1))),
                whole(width, HD),
                whole(width, HD),
            ],
            out_specs=[whole(answer, 1408)] * 4,
            scratch_shapes=[pltpu.VMEM((count * answer, width), BF)],
        ),
        out_shape=[out] * 4,
        compiler_params=pltpu.CompilerParams(vmem_limit_bytes=VMEM_LIMIT),
        cost_estimate=pl.CostEstimate(
            flops=2 * count * answer * width * 1280, bytes_accessed=9 << 20, transcendentals=0
        ),
        name="project",
    )(place, hidden, gain, w_query, w_key, w_value)


def attention_kernel(
    place, mask, p0, p1, p2, p3, cosine, sine,
    own_key, own_value, a1, a2, a3, b1, b2, b3,
    out, queries, near_key, near_value, keys, values, sem,
):
    section, core = place[0], place[1]
    answer = p0.shape[0]
    heads = out.shape[1] // HD
    local = own_key.shape[0]
    half = local // 2
    sections = keys.shape[0] // local

    copies = [
        pltpu.make_async_copy(
            own_key, keys.at[pl.ds(pl.multiple_of(section * local, local), local), pl.ds(0, HD)], sem.at[0]
        ),
        pltpu.make_async_copy(
            own_value, values.at[pl.ds(pl.multiple_of(section * local, local), local), pl.ds(0, HD)], sem.at[1]
        ),
    ]
    for r, (mine, other) in enumerate(((a1, b1), (a2, b2), (a3, b3)), 1):
        source = lax.rem(section + sections - r, sections)
        for piece, side, which in ((mine, core, 0), (other, 1 - core, 1)):
            start = pl.multiple_of(source * local + side * half, half)
            for kind, buffer in ((0, keys), (1, values)):
                copies.append(
                    pltpu.make_async_copy(
                        piece.at[kind],
                        buffer.at[pl.ds(start, half), pl.ds(0, HD)],
                        sem.at[4 * r - 2 + 2 * which + kind],
                    )
                )
    for copy in copies:
        copy.start()

    lane = lax.broadcasted_iota(jnp.int32, (256, HD), 1)
    first = jnp.where(lane == 0, 1.0, 0.0)

    def fill(b, carry):
        bias = jnp.where(mask[section, b] > 0, 0.0, masked_score)
        keys[pl.ds(pl.multiple_of(b * BLOCK, BLOCK), BLOCK), HD:] = jnp.full((BLOCK, HD), bias, F32).astype(BF)
        values[pl.ds(pl.multiple_of(b * BLOCK, BLOCK), BLOCK), HD:] = first[:BLOCK].astype(BF)
        return carry

    lax.fori_loop(0, keys.shape[0] // BLOCK, fill, 0, unroll=4)

    total = (
        p0[:, 1280:].astype(F32) + p1[:, 1280:].astype(F32)
        + p2[:, 1280:].astype(F32) + p3[:, 1280:].astype(F32)
    )
    scale = lax.rsqrt((total[:, 0:1] + total[:, 1:2]) / D + norm_eps)

    def column(h):
        at = slice(h * HD, (h + 1) * HD)
        return (
            p0[:, at].astype(F32) + p1[:, at].astype(F32)
            + p2[:, at].astype(F32) + p3[:, at].astype(F32)
        ) * scale

    def turned(x):
        return x * cosine[...] + pltpu.roll(x, HD // 2, 1) * sine[...]

    factor = math.log2(math.e) / math.sqrt(HD)
    for h in range(heads):
        queries[h * answer : (h + 1) * answer, :HD] = (turned(column(h)) * factor).astype(BF)
    for i in range(heads * answer // 256):
        queries[i * 256 : (i + 1) * 256, HD:] = first.astype(BF)
    near_key[...] = turned(column(heads)).astype(BF)
    near_value[:, :HD] = column(heads + 1).astype(BF)
    near_value[:, HD:] = first[:answer].astype(BF)

    for copy in copies:
        copy.wait()

    rows = 256
    tile = 1024
    dims = (((1,), (1,)), ((), ()))
    causal = lax.rem(lax.broadcasted_iota(jnp.int32, (rows, answer), 0), answer) >= (
        lax.broadcasted_iota(jnp.int32, (rows, answer), 1)
    )

    for block in range(heads * answer // rows):
        q = queries[block * rows : (block + 1) * rows, :HD]
        q=jnp.concatenate([q,first.astype(BF)],axis=1)
        s = lax.dot_general(q[:, :HD], near_key[...], dims, preferred_element_type=F32)
        s = jnp.where(causal, s, masked_score)
        m = jnp.max(s, axis=-1, keepdims=True)
        acc = jnp.dot(jnp.exp2(s - m).astype(BF), near_value[...], preferred_element_type=F32)

        def far(t, state):
            m, acc = state
            at = pl.ds(pl.multiple_of(t * tile, tile), tile)
            s = lax.dot_general(q, keys[at], dims, preferred_element_type=F32)
            m_new = jnp.maximum(m, jnp.max(s, axis=-1, keepdims=True))
            p = jnp.exp2(s - m_new).astype(BF)
            acc = acc * jnp.exp2(m - m_new) + jnp.dot(p, values[at], preferred_element_type=F32)
            return m_new, acc

        m, acc = lax.fori_loop(0, keys.shape[0] // tile, far, (m, acc), unroll=2)
        result = acc[:, :HD] / acc[:, HD : HD + 1]
        for j in range(rows // answer):
            h = block * (rows // answer) + j
            out[:, h * HD : (h + 1) * HD] = result[j * answer : (j + 1) * answer].astype(BF)


def attend(place, mask, parts, cosine, sine, own_key, own_value, mine, other):
    answer = parts[0].shape[0]
    context = NBLK * BLOCK
    heads = (parts[0].shape[1] - 3 * HD) // HD
    vmem = pl.BlockSpec(memory_space=pltpu.VMEM)
    smem = pl.BlockSpec(memory_space=pltpu.SMEM)
    anywhere = pl.BlockSpec(memory_space=pl.ANY)
    return pl.pallas_call(
        attention_kernel,
        in_specs=[smem, smem] + [vmem] * 6 + [anywhere] * 8,
        out_specs=vmem,
        out_shape=jax.ShapeDtypeStruct((answer, heads * HD), BF),
        scratch_shapes=[
            pltpu.VMEM((heads * answer, 2 * HD), BF),
            pltpu.VMEM((answer, HD), BF),
            pltpu.VMEM((answer, 2 * HD), BF),
            pltpu.VMEM((context, 2 * HD), BF),
            pltpu.VMEM((context, 2 * HD), BF),
            pltpu.SemaphoreType.DMA((14,)),
        ],
        compiler_params=pltpu.CompilerParams(vmem_limit_bytes=VMEM_LIMIT),
        cost_estimate=pl.CostEstimate(
            flops=8 * heads * answer * context * HD,
            bytes_accessed=6 << 20,
            transcendentals=heads * answer * context,
        ),
        name="attend",
    )(place, mask, *parts, cosine, sine, own_key, own_value, *mine, *other)


def output_kernel(place, a0, a1, a2, a3, w_out, o0, o1, o2, o3, rows):
    step = pl.program_id(0)
    count, answer, _ = rows.shape

    @pl.when(step == 0)
    def _():
        for r, part in enumerate((a0, a1, a2, a3)):
            rows[lax.rem(place[0] + count - r, count)] = part[...]

    product = jnp.dot(
        rows[...].reshape(count * answer, rows.shape[2]), w_out[...], preferred_element_type=F32
    )
    for k, out in enumerate((o0, o1, o2, o3)):

        @pl.when(step == k)
        def _():
            half = out.shape[2]
            out[0] = product[:, :half].astype(out.dtype)
            out[1] = product[:, half:].astype(out.dtype)


def project_out(place, parts, w_out):
    answer, depth = parts[0].shape
    width = w_out.shape[1] // 4
    whole = lambda *shape: pl.BlockSpec(shape, lambda i, place: (0,) * len(shape))
    shape = (2, 4 * answer, width // 2)
    return pl.pallas_call(
        output_kernel,
        grid_spec=pltpu.PrefetchScalarGridSpec(
            num_scalar_prefetch=1,
            grid=(4,),
            in_specs=[whole(answer, depth)] * 4
            + [pl.BlockSpec((depth, width), lambda i, place: (0, lax.rem(place[2] + i, 4)))],
            out_specs=[whole(*shape)] * 4,
            scratch_shapes=[pltpu.VMEM((4, answer, depth), BF)],
        ),
        out_shape=[jax.ShapeDtypeStruct(shape, F32)] + [jax.ShapeDtypeStruct(shape, BF)] * 3,
        compiler_params=pltpu.CompilerParams(vmem_limit_bytes=VMEM_LIMIT),
        cost_estimate=pl.CostEstimate(
            flops=8 * answer * depth * width * 4, bytes_accessed=9 << 20, transcendentals=0
        ),
        name="project_out",
    )(place, *parts, w_out)


def rotation(answer):
    half = HD // 2
    positions = (NBLK * BLOCK + jnp.arange(answer)).astype(F32)
    frequency = rope_base ** (-2.0 * jnp.arange(half).astype(F32) / HD)
    angles = positions[:, None] * frequency[None, :]
    cosine, sine = jnp.cos(angles), jnp.sin(angles)
    return jnp.concatenate([cosine, cosine], axis=1), jnp.concatenate([-sine, sine], axis=1)


def per_device(
    hidden, norm_gain, w_query, w_key, w_value, w_out, cache_key, cache_value, block_mask
):
    section = lax.axis_index("section")
    core = lax.rem(lax.axis_index("coal"), 2)
    tensor = lax.axis_index("tensor")
    z_hi = lax.rem(tensor, 2)
    place = jnp.stack([section, core, tensor // 2]).astype(jnp.int32)
    answer = hidden.shape[1]
    half = cache_key.shape[0] // 2
    piece = jnp.stack(
        [
            lax.dynamic_slice_in_dim(cache_key, core * half, half, 0),
            lax.dynamic_slice_in_dim(cache_value, core * half, half, 0),
        ]
    )
    mine = [section_shift(piece, r) for r in (1, 2, 3)]
    other = [core_swap(m) for m in mine]
    cosine, sine = rotation(answer)

    chunks = project(place, hidden, norm_gain[None, :], w_query, w_key, w_value)
    parts = [chunks[0]] + [section_shift(chunks[r], r) for r in (1, 2, 3)]
    attention = attend(
        place, block_mask, parts, cosine, sine, cache_key, cache_value, mine, other
    )
    rows = [attention] + [section_shift(attention, r) for r in (1, 2, 3)]
    sums = project_out(place, rows, w_out)
    pieces = [sums[0]] + [x_shift(sums[r], r) for r in (1, 2, 3)]

    def reduced(side):
        return sum(lax.dynamic_index_in_dim(p, side, 0, False).astype(F32) for p in pieces)

    arrived = z_swap(reduced(1 - z_hi).astype(BF))
    result = reduced(z_hi) + arrived.astype(F32)
    return result.astype(BF).reshape(hidden.shape[0], answer, -1)


def solution(mesh):
    return jax.shard_map(
        per_device,
        mesh=mesh,
        in_specs=(
            P("coal", None, "section"),
            P("section"),
            P("section", "tensor"),
            P("section", "tensor"),
            P("section", "tensor"),
            P("tensor", "section"),
            P("section", "tensor"),
            P("section", "tensor"),
            P("coal", None),
        ),
        out_specs=P("coal", None, ("section", "tensor")),
        check_vma=False,
    )
```

```python
import functools
import math

import jax
import jax.numpy as jnp
from jax import lax
from jax.experimental import pallas as pl
from jax.experimental.pallas import tpu as pltpu
from jax.sharding import PartitionSpec as P

D = 8192
HD = 128
NBLK = 128
BLOCK = 64
rope_base = 500000.0
norm_eps = 1e-05
masked_score = -1e30
BF = jnp.bfloat16
F32 = jnp.float32
HALVES = 2
MIB = 1024 * 1024


def section_shift(x, by):
    n = lax.axis_size("section")
    return lax.ppermute(x, "section", [(i, (i + by) % n) for i in range(n)])


def x_shift(x, by):
    n = lax.axis_size("tensor") // 2
    return lax.ppermute(
        x, "tensor", [(i, ((i // 2 + by) % n) * 2 + i % 2) for i in range(2 * n)]
    )


def z_swap(x):
    return lax.ppermute(x, "tensor", [(i, i ^ 1) for i in range(lax.axis_size("tensor"))])


def core_swap(x):
    return lax.ppermute(x, "coal", [(i, i ^ 1) for i in range(lax.axis_size("coal"))])


def project_kernel(place, hidden, gain, w_query, w_key, w_value, *rest):
    outs, (rows, weights, scaled, product, sem) = rest[:-5], rest[-5:]
    count, answer, width = hidden.shape
    queries = w_query.shape[1]
    span = answer // HALVES
    steps, _, _, depth = rows.shape
    copies = []
    for k in range(steps):
        at = pl.ds(k * depth, depth)
        group = [
            (hidden.at[lax.rem(place[0] + r, count), :, at], rows.at[k, r]) for r in range(count)
        ]
        group += [
            (w_query.at[at], weights.at[at, pl.ds(0, queries)]),
            (w_key.at[at], weights.at[at, pl.ds(queries, HD)]),
            (w_value.at[at], weights.at[at, pl.ds(queries + HD, HD)]),
        ]
        copies.append(
            [pltpu.make_async_copy(a, b, sem.at[k, i]) for i, (a, b) in enumerate(group)]
        )
        for copy in copies[-1]:
            copy.start()

    squares = [jnp.zeros((answer, 128), F32) for _ in range(count)]
    for k in range(steps):
        at = slice(k * depth, (k + 1) * depth)
        for copy in copies[k]:
            copy.wait()
        for r in range(count):
            x = rows[k, r].astype(F32)
            x2 = x * x
            for j in range(depth // 128):
                squares[r] = squares[r] + x2[:, j * 128 : (j + 1) * 128]
            scaled[k, r * answer : (r + 1) * answer] = (x * gain[:, at]).astype(BF)
        partial = jnp.dot(scaled[k], weights[at], preferred_element_type=F32)
        if k == 0:
            product[...] = partial
        elif k < steps - 1:
            product[...] += partial
        else:
            partial = product[...] + partial
            lane = lax.broadcasted_iota(jnp.int32, (answer, 128), 1)
            for r in range(count):
                total = jnp.sum(squares[r], axis=-1, keepdims=True)
                high = total.astype(BF).astype(F32)
                pair = jnp.where(lane == 0, high, jnp.where(lane == 1, total - high, 0.0))
                for h in range(HALVES):
                    out = outs[r * HALVES + h]
                    start = r * answer + h * span
                    out[:, : queries + 2 * HD] = partial[start : start + span].astype(BF)
                    out[:, queries + 2 * HD :] = pair[h * span : (h + 1) * span].astype(BF)


def project(place, hidden, gain, w_query, w_key, w_value):
    count, answer, width = hidden.shape
    total = w_query.shape[1] + 2 * HD
    steps = 4
    smem = pl.BlockSpec(memory_space=pltpu.SMEM)
    vmem = pl.BlockSpec(memory_space=pltpu.VMEM)
    anywhere = pl.BlockSpec(memory_space=pl.ANY)
    return pl.pallas_call(
        project_kernel,
        in_specs=[smem, anywhere, vmem, anywhere, anywhere, anywhere],
        out_specs=[vmem] * (count * HALVES),
        out_shape=[jax.ShapeDtypeStruct((answer // HALVES, total + HD), BF)] * (count * HALVES),
        scratch_shapes=[
            pltpu.VMEM((steps, count, answer, width // steps), BF),
            pltpu.VMEM((width, total), BF),
            pltpu.VMEM((steps, count * answer, width // steps), BF),
            pltpu.VMEM((count * answer, total), F32),
            pltpu.SemaphoreType.DMA((steps, count + 3)),
        ],
        compiler_params=pltpu.CompilerParams(vmem_limit_bytes=32 * MIB),
        cost_estimate=pl.CostEstimate(
            flops=2 * count * answer * width * total, bytes_accessed=9 * MIB, transcendentals=0
        ),
        name="project",
    )(place, hidden, gain, w_query, w_key, w_value)


def attention_kernel(half, place, mask, p0, p1, p2, p3, cosine, sine, *rest):
    before, rest = (rest[:2], rest[2:]) if half else ((), rest)
    own_key, own_value, a1, a2, a3, b1, b2, b3, out, *rest = rest
    after, rest = ([], rest) if half == HALVES - 1 else (rest[:2], rest[2:])
    queries, near_key, near_value, keys, values, buf0, buf1, sem = rest
    buffers = (buf0, buf1)
    section, core = place[0], place[1]
    span = p0.shape[0]
    answer = near_key.shape[0]
    heads = out.shape[1] // HD
    rows = heads * span
    local = own_key.shape[0]
    piece_rows = local // 2
    sections = keys.shape[0] // local

    copies = []

    def bring(source, buffer, start, size):
        copy = pltpu.make_async_copy(
            source,
            buffer.at[pl.ds(pl.multiple_of(start, size), size), pl.ds(0, HD)],
            sem.at[len(copies)],
        )
        copy.start()
        copies.append(copy)

    bring(own_key, keys, section * local, local)
    bring(own_value, values, section * local, local)
    for r, pieces in enumerate(((a1, b1), (a2, b2), (a3, b3)), 1):
        source = lax.rem(section + sections - r, sections)
        for piece, side in zip(pieces, (core, 1 - core)):
            for kind, buffer in ((0, keys), (1, values)):
                bring(piece.at[kind], buffer, source * local + side * piece_rows, piece_rows)

    first = jnp.where(lax.broadcasted_iota(jnp.int32, (rows, HD), 1) == 0, 1.0, 0.0).astype(BF)

    def fill(b, carry):
        at = pl.ds(pl.multiple_of(b * BLOCK, BLOCK), BLOCK)
        bias = jnp.where(mask[section, b] > 0, 0.0, masked_score)
        keys[at, HD:] = jnp.full((BLOCK, HD), bias, F32).astype(BF)
        values[at, HD:] = first[:BLOCK]
        return carry

    lax.fori_loop(0, keys.shape[0] // BLOCK, fill, 0, unroll=4)

    width = (heads + 2) * HD
    total = (
        p0[:, width:].astype(F32) + p1[:, width:].astype(F32)
        + p2[:, width:].astype(F32) + p3[:, width:].astype(F32)
    )
    scale = lax.rsqrt((total[:, 0:1] + total[:, 1:2]) / D + norm_eps)

    def column(h):
        at = slice(h * HD, (h + 1) * HD)
        return (
            p0[:, at].astype(F32) + p1[:, at].astype(F32)
            + p2[:, at].astype(F32) + p3[:, at].astype(F32)
        ) * scale

    def turned(x):
        return x * cosine[...] + pltpu.roll(x, HD // 2, 1) * sine[...]

    factor = math.log2(math.e) / math.sqrt(HD)
    for h in range(heads):
        queries[h * span : (h + 1) * span] = (turned(column(h)) * factor).astype(BF)
    new_key = turned(column(heads)).astype(BF)
    new_value = column(heads + 1).astype(BF)
    for ref, new in zip(after, (new_key, new_value)):
        ref[...] = new
    near_value[:, HD:] = first[:answer]
    for h in range(HALVES):
        at = slice(h * span, (h + 1) * span)
        if h == half:
            near_key[at], near_value[at, :HD] = new_key, new_value
        elif h < half:
            near_key[at], near_value[at, :HD] = before[0][...], before[1][...]
        else:
            near_key[at] = jnp.zeros((span, HD), BF)
            near_value[at, :HD] = jnp.zeros((span, HD), BF)

    tile = 1024
    tiles = keys.shape[0] // tile
    dims = (((1,), (1,)), ((), ()))
    q = queries[...]
    q_aug = jnp.concatenate([q, first], axis=1)
    s = lax.dot_general(q, near_key[...], dims, preferred_element_type=F32)
    row = lax.rem(lax.broadcasted_iota(jnp.int32, (rows, answer), 0), span) + half * span
    s = jnp.where(row >= lax.broadcasted_iota(jnp.int32, (rows, answer), 1), s, masked_score)
    m = jnp.max(s, axis=-1, keepdims=True)
    acc = jnp.dot(jnp.exp2(s - m).astype(BF), near_value[...], preferred_element_type=F32)

    for copy in copies:
        copy.wait()

    def score(t):
        s = lax.dot_general(
            q_aug, keys[t * tile : (t + 1) * tile], dims, preferred_element_type=F32
        )
        buffers[t % 2][...] = s
        return jnp.max(s, axis=-1, keepdims=True)

    top = score(0)
    for t in range(tiles):
        m_new = jnp.maximum(m, top)
        if t + 1 < tiles:
            top = score(t + 1)
        p = jnp.exp2(buffers[t % 2][...] - m_new).astype(BF)
        acc = acc * jnp.exp2(m - m_new) + jnp.dot(
            p, values[t * tile : (t + 1) * tile], preferred_element_type=F32
        )
        m = m_new
    result = (acc[:, :HD] / acc[:, HD : HD + 1]).astype(BF)
    for h in range(heads):
        out[:, h * HD : (h + 1) * HD] = result[h * span : (h + 1) * span]


def attend(half, place, mask, parts, cosine, sine, before, own_key, own_value, mine, other):
    span = parts[0].shape[0]
    answer = span * HALVES
    context = NBLK * BLOCK
    heads = parts[0].shape[1] // HD - 3
    rows = heads * span
    vmem = pl.BlockSpec(memory_space=pltpu.VMEM)
    smem = pl.BlockSpec(memory_space=pltpu.SMEM)
    anywhere = pl.BlockSpec(memory_space=pl.ANY)
    extra = 0 if half == HALVES - 1 else 2
    outs = [jax.ShapeDtypeStruct((span, heads * HD), BF)]
    outs += [jax.ShapeDtypeStruct((span, HD), BF)] * extra
    return pl.pallas_call(
        functools.partial(attention_kernel, half),
        in_specs=[smem, smem] + [vmem] * (6 + len(before)) + [anywhere] * 8,
        out_specs=[vmem] * (1 + extra),
        out_shape=outs,
        scratch_shapes=[
            pltpu.VMEM((rows, HD), BF),
            pltpu.VMEM((answer, HD), BF),
            pltpu.VMEM((answer, 2 * HD), BF),
            pltpu.VMEM((context, 2 * HD), BF),
            pltpu.VMEM((context, 2 * HD), BF),
            pltpu.VMEM((rows, 1024), F32),
            pltpu.VMEM((rows, 1024), F32),
            pltpu.SemaphoreType.DMA((14,)),
        ],
        compiler_params=pltpu.CompilerParams(vmem_limit_bytes=32 * MIB),
        cost_estimate=pl.CostEstimate(
            flops=8 * rows * context * HD,
            bytes_accessed=6 * MIB,
            transcendentals=rows * context,
        ),
        name="attend",
    )(place, mask, *parts, cosine, sine, *before, own_key, own_value, *mine, *other)


def output_kernel(place, a0, a1, a2, a3, w_out, o0, o1, o2, o3, rows, weights, sem):
    count, span, depth = rows.shape
    outs = (o0, o1, o2, o3)
    width = w_out.shape[1] // len(outs)
    copies = []
    for k in range(len(outs)):
        at = pl.ds(pl.multiple_of(lax.rem(place[2] + k, len(outs)) * width, width), width)
        copies.append(pltpu.make_async_copy(w_out.at[:, at], weights.at[k], sem.at[k]))
        copies[-1].start()
    for r, part in enumerate((a0, a1, a2, a3)):
        rows[lax.rem(place[0] + count - r, count)] = part[...]
    left = rows[...].reshape(count * span, depth)
    for k, out in enumerate(outs):
        copies[k].wait()
        for side in range(2):
            at = slice(side * width // 2, (side + 1) * width // 2)
            out[side] = jnp.dot(left, weights[k, :, at], preferred_element_type=F32).astype(
                out.dtype
            )


def project_out(place, parts, w_out):
    span, depth = parts[0].shape
    count = len(parts)
    width = w_out.shape[1] // 4
    vmem = pl.BlockSpec(memory_space=pltpu.VMEM)
    smem = pl.BlockSpec(memory_space=pltpu.SMEM)
    shape = (2, count * span, width // 2)
    return pl.pallas_call(
        output_kernel,
        in_specs=[smem] + [vmem] * count + [pl.BlockSpec(memory_space=pl.ANY)],
        out_specs=[vmem] * 4,
        out_shape=[jax.ShapeDtypeStruct(shape, F32)] + [jax.ShapeDtypeStruct(shape, BF)] * 3,
        scratch_shapes=[
            pltpu.VMEM((count, span, depth), BF),
            pltpu.VMEM((4, depth, width), BF),
            pltpu.SemaphoreType.DMA((4,)),
        ],
        compiler_params=pltpu.CompilerParams(vmem_limit_bytes=24 * MIB),
        cost_estimate=pl.CostEstimate(
            flops=8 * count * span * depth * width, bytes_accessed=6 * MIB, transcendentals=0
        ),
        name="project_out",
    )(place, *parts, w_out)


def rotation(answer):
    half = HD // 2
    positions = (NBLK * BLOCK + jnp.arange(answer)).astype(F32)
    frequency = rope_base ** (-2.0 * jnp.arange(half).astype(F32) / HD)
    angles = positions[:, None] * frequency[None, :]
    cosine, sine = jnp.cos(angles), jnp.sin(angles)
    return jnp.concatenate([cosine, cosine], axis=1), jnp.concatenate([-sine, sine], axis=1)


def per_device(
    hidden, norm_gain, w_query, w_key, w_value, w_out, cache_key, cache_value, block_mask
):
    section = lax.axis_index("section")
    core = lax.rem(lax.axis_index("coal"), 2)
    tensor = lax.axis_index("tensor")
    z_hi = lax.rem(tensor, 2)
    place = jnp.stack([section, core, tensor // 2]).astype(jnp.int32)
    answer = hidden.shape[1]
    span = answer // HALVES
    half_rows = cache_key.shape[0] // 2
    piece = jnp.stack(
        [
            lax.dynamic_slice_in_dim(cache_key, core * half_rows, half_rows, 0),
            lax.dynamic_slice_in_dim(cache_value, core * half_rows, half_rows, 0),
        ]
    )
    mine = [section_shift(piece, r) for r in (1, 2, 3)]
    other = [core_swap(m) for m in mine]
    cosine, sine = rotation(answer)

    chunks = project(place, hidden, norm_gain[None, :], w_query, w_key, w_value)
    parts = [
        [chunks[h]] + [section_shift(chunks[r * HALVES + h], r) for r in (1, 2, 3)]
        for h in range(HALVES)
    ]
    before, sums = [], []
    for h in range(HALVES):
        at = slice(h * span, (h + 1) * span)
        attention, *before = attend(
            h, place, block_mask, parts[h], cosine[at], sine[at], before,
            cache_key, cache_value, mine, other,
        )
        rows = [attention] + [section_shift(attention, r) for r in (1, 2, 3)]
        sums.append(project_out(place, rows, w_out))

    results = []
    for h in range(HALVES):
        pieces = [sums[h][0]] + [x_shift(sums[h][r], r) for r in (1, 2, 3)]

        def reduced(side):
            return sum(lax.dynamic_index_in_dim(p, side, 0, False).astype(F32) for p in pieces)

        arrived = z_swap(reduced(1 - z_hi).astype(BF))
        result = reduced(z_hi) + arrived.astype(F32)
        results.append(result.astype(BF).reshape(hidden.shape[0], span, -1))
    return jnp.concatenate(results, axis=1)


def solution(mesh):
    return jax.shard_map(
        per_device,
        mesh=mesh,
        in_specs=(
            P("coal", None, "section"),
            P("section"),
            P("section", "tensor"),
            P("section", "tensor"),
            P("section", "tensor"),
            P("tensor", "section"),
            P("section", "tensor"),
            P("section", "tensor"),
            P("coal", None),
        ),
        out_specs=P("coal", None, ("section", "tensor")),
        check_vma=False,
    )
```

```python
import functools
import math

import jax
import jax.numpy as jnp
from jax import lax
from jax.experimental import pallas as pl
from jax.experimental.pallas import tpu as pltpu
from jax.sharding import PartitionSpec as P

D = 8192
HD = 128
NBLK = 128
BLOCK = 64
rope_base = 500000.0
norm_eps = 1e-05
masked_score = -1e30
BF = jnp.bfloat16
F32 = jnp.float32
HALVES = 2
TILE = 1024
MIB = 1024 * 1024


def section_shift(x, by):
    n = lax.axis_size("section")
    return lax.ppermute(x, "section", [(i, (i + by) % n) for i in range(n)])


def x_shift(x, by):
    n = lax.axis_size("tensor") // 2
    return lax.ppermute(
        x, "tensor", [(i, ((i // 2 + by) % n) * 2 + i % 2) for i in range(2 * n)]
    )


def z_swap(x):
    return lax.ppermute(x, "tensor", [(i, i ^ 1) for i in range(lax.axis_size("tensor"))])


def core_swap(x):
    return lax.ppermute(x, "coal", [(i, i ^ 1) for i in range(lax.axis_size("coal"))])


def project_kernel(place, hidden, gain, w_query, w_key, w_value, *rest):
    outs, (rows, weights, scaled, product, sem) = rest[:-5], rest[-5:]
    count, answer, width = hidden.shape
    queries = w_query.shape[1]
    span = answer // HALVES
    steps, _, _, depth = rows.shape
    copies = []
    for k in range(steps):
        at = pl.ds(k * depth, depth)
        group = [
            (hidden.at[lax.rem(place[0] + r, count), :, at], rows.at[k, r]) for r in range(count)
        ]
        group += [
            (w_query.at[at], weights.at[at, pl.ds(0, queries)]),
            (w_key.at[at], weights.at[at, pl.ds(queries, HD)]),
            (w_value.at[at], weights.at[at, pl.ds(queries + HD, HD)]),
        ]
        copies.append(
            [pltpu.make_async_copy(a, b, sem.at[k, i]) for i, (a, b) in enumerate(group)]
        )
        for copy in copies[-1]:
            copy.start()

    squares = [jnp.zeros((answer, 128), F32) for _ in range(count)]
    for k in range(steps):
        at = slice(k * depth, (k + 1) * depth)
        for copy in copies[k]:
            copy.wait()
        for r in range(count):
            x = rows[k, r].astype(F32)
            x2 = x * x
            for j in range(depth // 128):
                squares[r] = squares[r] + x2[:, j * 128 : (j + 1) * 128]
            scaled[k, r * answer : (r + 1) * answer] = (x * gain[:, at]).astype(BF)
        partial = jnp.dot(scaled[k], weights[at], preferred_element_type=F32)
        if k == 0:
            product[...] = partial
        elif k < steps - 1:
            product[...] += partial
        else:
            partial = product[...] + partial
            lane = lax.broadcasted_iota(jnp.int32, (answer, 128), 1)
            for r in range(count):
                total = jnp.sum(squares[r], axis=-1, keepdims=True)
                high = total.astype(BF).astype(F32)
                pair = jnp.where(lane == 0, high, jnp.where(lane == 1, total - high, 0.0))
                for h in range(HALVES):
                    out = outs[r * HALVES + h]
                    start = r * answer + h * span
                    out[:, : queries + 2 * HD] = partial[start : start + span].astype(BF)
                    out[:, queries + 2 * HD :] = pair[h * span : (h + 1) * span].astype(BF)


def project(place, hidden, gain, w_query, w_key, w_value):
    count, answer, width = hidden.shape
    total = w_query.shape[1] + 2 * HD
    steps = 4
    smem = pl.BlockSpec(memory_space=pltpu.SMEM)
    vmem = pl.BlockSpec(memory_space=pltpu.VMEM)
    anywhere = pl.BlockSpec(memory_space=pl.ANY)
    return pl.pallas_call(
        project_kernel,
        in_specs=[smem, anywhere, vmem, anywhere, anywhere, anywhere],
        out_specs=[vmem] * (count * HALVES),
        out_shape=[jax.ShapeDtypeStruct((answer // HALVES, total + HD), BF)] * (count * HALVES),
        scratch_shapes=[
            pltpu.VMEM((steps, count, answer, width // steps), BF),
            pltpu.VMEM((width, total), BF),
            pltpu.VMEM((steps, count * answer, width // steps), BF),
            pltpu.VMEM((count * answer, total), F32),
            pltpu.SemaphoreType.DMA((steps, count + 3)),
        ],
        compiler_params=pltpu.CompilerParams(vmem_limit_bytes=60 * MIB),
        cost_estimate=pl.CostEstimate(
            flops=2 * count * answer * width * total, bytes_accessed=9 * MIB, transcendentals=0
        ),
        name="project",
    )(place, hidden, gain, w_query, w_key, w_value)


def attention_kernel(half, place, mask, p0, p1, p2, p3, cosine, sine, *rest):
    before, rest = (rest[:2], rest[2:]) if half else ((), rest)
    own_key, own_value, a1, a2, a3, b1, b2, b3, out, *rest = rest
    after, rest = ([], rest) if half == HALVES - 1 else (rest[:2], rest[2:])
    queries, near_key, near_value, keys, values, buf0, buf1, sem = rest
    section, core = place[0], place[1]
    span = p0.shape[0]
    answer = near_key.shape[0]
    heads = out.shape[1] // HD
    rows = heads * span
    local = own_key.shape[0]
    piece_rows = local // 2
    sections = keys.shape[0] // local

    copies = []

    def bring(source, buffer, start, size):
        copy = pltpu.make_async_copy(
            source,
            buffer.at[pl.ds(pl.multiple_of(start, size), size), pl.ds(0, HD)],
            sem.at[len(copies)],
        )
        copy.start()
        copies.append(copy)

    bring(own_key, keys, section * local, local)
    bring(own_value, values, section * local, local)
    for r, pieces in enumerate(((a1, b1), (a2, b2), (a3, b3)), 1):
        source = lax.rem(section + sections - r, sections)
        for piece, side in zip(pieces, (core, 1 - core)):
            for kind, buffer in ((0, keys), (1, values)):
                bring(piece.at[kind], buffer, source * local + side * piece_rows, piece_rows)

    first = jnp.where(lax.broadcasted_iota(jnp.int32, (rows, HD), 1) == 0, 1.0, 0.0).astype(BF)

    def fill(b, carry):
        at = pl.ds(pl.multiple_of(b * BLOCK, BLOCK), BLOCK)
        bias = jnp.where(mask[section, b] > 0, 0.0, masked_score)
        keys[at, HD:] = jnp.full((BLOCK, HD), bias, F32).astype(BF)
        values[at, HD:] = first[:BLOCK]
        return carry

    lax.fori_loop(0, keys.shape[0] // BLOCK, fill, 0, unroll=4)

    width = (heads + 2) * HD
    total = (
        p0[:, width:].astype(F32) + p1[:, width:].astype(F32)
        + p2[:, width:].astype(F32) + p3[:, width:].astype(F32)
    )
    scale = lax.rsqrt((total[:, 0:1] + total[:, 1:2]) / D + norm_eps)

    def column(h):
        at = slice(h * HD, (h + 1) * HD)
        return (
            p0[:, at].astype(F32) + p1[:, at].astype(F32)
            + p2[:, at].astype(F32) + p3[:, at].astype(F32)
        ) * scale

    def turned(x):
        return x * cosine[...] + pltpu.roll(x, HD // 2, 1) * sine[...]

    factor = math.log2(math.e) / math.sqrt(HD)
    for h in range(heads):
        queries[h * span : (h + 1) * span] = (turned(column(h)) * factor).astype(BF)
    new_key = turned(column(heads)).astype(BF)
    new_value = column(heads + 1).astype(BF)
    for ref, new in zip(after, (new_key, new_value)):
        ref[...] = new
    near_value[:, HD:] = first[:answer]
    for h in range(HALVES):
        at = slice(h * span, (h + 1) * span)
        if h == half:
            near_key[at], near_value[at, :HD] = new_key, new_value
        elif h < half:
            near_key[at], near_value[at, :HD] = before[0][...], before[1][...]
        else:
            near_key[at] = jnp.zeros((span, HD), BF)
            near_value[at, :HD] = jnp.zeros((span, HD), BF)

    tile = buf0.shape[1]
    tiles = keys.shape[0] // tile
    dims = (((1,), (1,)), ((), ()))
    q = queries[...]
    q_aug = jnp.concatenate([q, first], axis=1)
    s = lax.dot_general(q, near_key[...], dims, preferred_element_type=F32)
    row = lax.rem(lax.broadcasted_iota(jnp.int32, (rows, answer), 0), span) + half * span
    s = jnp.where(row >= lax.broadcasted_iota(jnp.int32, (rows, answer), 1), s, masked_score)
    m = jnp.max(s, axis=-1, keepdims=True)
    acc = jnp.dot(jnp.exp2(s - m).astype(BF), near_value[...], preferred_element_type=F32)

    for copy in copies:
        copy.wait()

    def score(t, buffer):
        at = pl.ds(pl.multiple_of(t * tile, tile), tile)
        s = lax.dot_general(q_aug, keys[at], dims, preferred_element_type=F32)
        buffer[...] = s
        return jnp.max(s, axis=-1, keepdims=True)

    def weigh(t, buffer, m, m_new, acc):
        at = pl.ds(pl.multiple_of(t * tile, tile), tile)
        p = jnp.exp2(buffer[...] - m_new).astype(BF)
        return acc * jnp.exp2(m - m_new) + jnp.dot(p, values[at], preferred_element_type=F32)

    def pair(i, state):
        m, top, acc = state
        t = 2 * i
        m_new = jnp.maximum(m, top)
        top = score(t + 1, buf1)
        acc = weigh(t, buf0, m, m_new, acc)
        m = m_new
        m_new = jnp.maximum(m, top)
        top = score(lax.rem(t + 2, tiles), buf0)
        acc = weigh(t + 1, buf1, m, m_new, acc)
        return m_new, top, acc

    m, _, acc = lax.fori_loop(0, tiles // 2, pair, (m, score(0, buf0), acc))
    result = (acc[:, :HD] / acc[:, HD : HD + 1]).astype(BF)
    for h in range(heads):
        out[:, h * HD : (h + 1) * HD] = result[h * span : (h + 1) * span]


def attend(half, place, mask, parts, cosine, sine, before, own_key, own_value, mine, other):
    span = parts[0].shape[0]
    answer = span * HALVES
    context = NBLK * BLOCK
    heads = parts[0].shape[1] // HD - 3
    rows = heads * span
    vmem = pl.BlockSpec(memory_space=pltpu.VMEM)
    smem = pl.BlockSpec(memory_space=pltpu.SMEM)
    anywhere = pl.BlockSpec(memory_space=pl.ANY)
    extra = 0 if half == HALVES - 1 else 2
    outs = [jax.ShapeDtypeStruct((span, heads * HD), BF)]
    outs += [jax.ShapeDtypeStruct((span, HD), BF)] * extra
    return pl.pallas_call(
        functools.partial(attention_kernel, half),
        in_specs=[smem, smem] + [vmem] * (6 + len(before)) + [anywhere] * 8,
        out_specs=[vmem] * (1 + extra),
        out_shape=outs,
        scratch_shapes=[
            pltpu.VMEM((rows, HD), BF),
            pltpu.VMEM((answer, HD), BF),
            pltpu.VMEM((answer, 2 * HD), BF),
            pltpu.VMEM((context, 2 * HD), BF),
            pltpu.VMEM((context, 2 * HD), BF),
            pltpu.VMEM((rows, TILE), F32),
            pltpu.VMEM((rows, TILE), F32),
            pltpu.SemaphoreType.DMA((14,)),
        ],
        compiler_params=pltpu.CompilerParams(vmem_limit_bytes=32 * MIB),
        cost_estimate=pl.CostEstimate(
            flops=8 * rows * context * HD,
            bytes_accessed=6 * MIB,
            transcendentals=rows * context,
        ),
        name="attend",
    )(place, mask, *parts, cosine, sine, *before, own_key, own_value, *mine, *other)


def output_kernel(place, a0, a1, a2, a3, w_out, before, o0, o1, o2, o3, after, rows, weights, sem):
    count, span, depth = rows.shape
    outs = (o0, o1, o2, o3)
    after[...] = jnp.zeros_like(after)
    width = w_out.shape[1] // len(outs)
    copies = []
    for k in range(len(outs)):
        at = pl.ds(pl.multiple_of(lax.rem(place[2] + k, len(outs)) * width, width), width)
        copies.append(pltpu.make_async_copy(w_out.at[:, at], weights.at[k], sem.at[k]))
        copies[-1].start()
    for r, part in enumerate((a0, a1, a2, a3)):
        rows[lax.rem(place[0] + count - r, count)] = part[...]
    left = rows[...].reshape(count * span, depth)
    for k, out in enumerate(outs):
        copies[k].wait()
        for side in range(2):
            at = slice(side * width // 2, (side + 1) * width // 2)
            out[side] = jnp.dot(left, weights[k, :, at], preferred_element_type=F32).astype(
                out.dtype
            )


def project_out(place, parts, w_out, before):
    span, depth = parts[0].shape
    count = len(parts)
    width = w_out.shape[1] // 4
    vmem = pl.BlockSpec(memory_space=pltpu.VMEM)
    smem = pl.BlockSpec(memory_space=pltpu.SMEM)
    shape = (2, count * span, width // 2)
    return pl.pallas_call(
        output_kernel,
        in_specs=[smem] + [vmem] * count + [pl.BlockSpec(memory_space=pl.ANY)] * 2,
        out_specs=[vmem] * 5,
        out_shape=[jax.ShapeDtypeStruct(shape, F32)]
        + [jax.ShapeDtypeStruct(shape, BF)] * 3
        + [jax.ShapeDtypeStruct((8, 128), F32)],
        scratch_shapes=[
            pltpu.VMEM((count, span, depth), BF),
            pltpu.VMEM((4, depth, width), BF),
            pltpu.SemaphoreType.DMA((4,)),
        ],
        compiler_params=pltpu.CompilerParams(vmem_limit_bytes=24 * MIB),
        cost_estimate=pl.CostEstimate(
            flops=8 * count * span * depth * width, bytes_accessed=6 * MIB, transcendentals=0
        ),
        name="project_out",
    )(place, *parts, w_out, before)


def reduce_kernel(place, *refs):
    pieces, (send, keep) = refs[:-2], refs[-2:]
    each = len(pieces) // HALVES
    count, answer, _ = keep.shape
    span = answer // HALVES
    for h in range(HALVES):
        group = pieces[h * each : (h + 1) * each]
        for side, out in ((1 - place[3], send), (place[3], keep)):
            total = group[0][side].astype(F32)
            for piece in group[1:]:
                total = total + piece[side].astype(F32)
            for c in range(count):
                out[c, h * span : (h + 1) * span] = total[c * span : (c + 1) * span].astype(
                    out.dtype
                )


def reduce_pieces(place, pieces, count):
    _, rows, width = pieces[0].shape
    answer = rows // count * HALVES
    vmem = pl.BlockSpec(memory_space=pltpu.VMEM)
    return pl.pallas_call(
        reduce_kernel,
        in_specs=[pl.BlockSpec(memory_space=pltpu.SMEM)] + [vmem] * len(pieces),
        out_specs=[vmem] * 2,
        out_shape=[
            jax.ShapeDtypeStruct((count, answer, width), BF),
            jax.ShapeDtypeStruct((count, answer, width), F32),
        ],
        compiler_params=pltpu.CompilerParams(vmem_limit_bytes=16 * MIB),
        cost_estimate=pl.CostEstimate(
            flops=16 * rows * width, bytes_accessed=32 * rows * width, transcendentals=0
        ),
        name="reduce_pieces",
    )(place, *pieces)


def rotation(answer):
    half = HD // 2
    positions = (NBLK * BLOCK + jnp.arange(answer)).astype(F32)
    frequency = rope_base ** (-2.0 * jnp.arange(half).astype(F32) / HD)
    angles = positions[:, None] * frequency[None, :]
    cosine, sine = jnp.cos(angles), jnp.sin(angles)
    return jnp.concatenate([cosine, cosine], axis=1), jnp.concatenate([-sine, sine], axis=1)


def per_device(
    hidden, norm_gain, w_query, w_key, w_value, w_out, cache_key, cache_value, block_mask
):
    section = lax.axis_index("section")
    core = lax.rem(lax.axis_index("coal"), 2)
    tensor = lax.axis_index("tensor")
    z_hi = lax.rem(tensor, 2)
    place = jnp.stack([section, core, tensor // 2, z_hi]).astype(jnp.int32)
    answer = hidden.shape[1]
    span = answer // HALVES
    half_rows = cache_key.shape[0] // 2
    piece = jnp.stack(
        [
            lax.dynamic_slice_in_dim(cache_key, core * half_rows, half_rows, 0),
            lax.dynamic_slice_in_dim(cache_value, core * half_rows, half_rows, 0),
        ]
    )
    with jax.named_scope("cache"):
        mine = [section_shift(piece, r) for r in (1, 2, 3)]
    with jax.named_scope("swap"):
        other = [core_swap(m) for m in mine]
    cosine, sine = rotation(answer)

    chunks = project(place, hidden, norm_gain[None, :], w_query, w_key, w_value)
    parts = []
    for h in range(HALVES):
        with jax.named_scope(f"sums{h}"):
            parts.append(
                [chunks[h]] + [section_shift(chunks[r * HALVES + h], r) for r in (1, 2, 3)]
            )
    before, attended, gathered = [], [], []
    for h in range(HALVES):
        at = slice(h * span, (h + 1) * span)
        attention, *before = attend(
            h, place, block_mask, parts[h], cosine[at], sine[at], before,
            cache_key, cache_value, mine, other,
        )
        attended.append(attention)
        with jax.named_scope(f"gather{h}"):
            gathered.append([attention] + [section_shift(attention, r) for r in (1, 2, 3)])

    pieces = []
    turn = attended[-1]
    for h in range(HALVES):
        *sums, turn = project_out(place, gathered[h], w_out, turn)
        with jax.named_scope(f"x{h}"):
            pieces += [sums[0]] + [x_shift(sums[r], r) for r in (1, 2, 3)]
    send, keep = reduce_pieces(place, pieces, hidden.shape[0])
    with jax.named_scope("z"):
        arrived = z_swap(send)
    return (keep + arrived.astype(F32)).astype(BF)


def solution(mesh):
    return jax.shard_map(
        per_device,
        mesh=mesh,
        in_specs=(
            P("coal", None, "section"),
            P("section"),
            P("section", "tensor"),
            P("section", "tensor"),
            P("section", "tensor"),
            P("tensor", "section"),
            P("section", "tensor"),
            P("section", "tensor"),
            P("coal", None),
        ),
        out_specs=P("coal", None, ("section", "tensor")),
        check_vma=False,
    )
```

```python
import functools
import math

import jax
import jax.numpy as jnp
from jax import lax
from jax.experimental import pallas as pl
from jax.experimental.pallas import tpu as pltpu
from jax.sharding import PartitionSpec as P

D = 8192
HD = 128
NBLK = 128
BLOCK = 64
rope_base = 500000.0
norm_eps = 1e-05
masked_score = -1e30
BF = jnp.bfloat16
F32 = jnp.float32
HALVES = 2
TILE = 1024
ANSWER = 128
MIB = 1024 * 1024


def section_shift(x, by):
    n = lax.axis_size("section")
    return lax.ppermute(x, "section", [(i, (i + by) % n) for i in range(n)])


def x_shift(x, by):
    n = lax.axis_size("tensor") // 2
    return lax.ppermute(
        x, "tensor", [(i, ((i // 2 + by) % n) * 2 + i % 2) for i in range(2 * n)]
    )


def z_swap(x):
    return lax.ppermute(x, "tensor", [(i, i ^ 1) for i in range(lax.axis_size("tensor"))])


def core_swap(x):
    return lax.ppermute(x, "coal", [(i, i ^ 1) for i in range(lax.axis_size("coal"))])


def project_kernel(place, hidden, gain, w_query, w_key, w_value, *rest):
    outs, (rows, weights, scaled, product, sem) = rest[:-5], rest[-5:]
    count, answer, width = hidden.shape
    queries = w_query.shape[1]
    steps, _, _, depth = rows.shape
    copies = []
    for k in range(steps):
        at = pl.ds(k * depth, depth)
        group = [
            (hidden.at[lax.rem(place[0] + r, count), :, at], rows.at[k, r]) for r in range(count)
        ]
        group += [
            (w_query.at[at], weights.at[at, pl.ds(0, queries)]),
            (w_key.at[at], weights.at[at, pl.ds(queries, HD)]),
            (w_value.at[at], weights.at[at, pl.ds(queries + HD, HD)]),
        ]
        copies.append(
            [pltpu.make_async_copy(a, b, sem.at[k, i]) for i, (a, b) in enumerate(group)]
        )
        for copy in copies[-1]:
            copy.start()

    squares = [jnp.zeros((answer, 128), F32) for _ in range(count)]
    for k in range(steps):
        at = slice(k * depth, (k + 1) * depth)
        for copy in copies[k]:
            copy.wait()
        for r in range(count):
            x = rows[k, r].astype(F32)
            x2 = x * x
            for j in range(depth // 128):
                squares[r] = squares[r] + x2[:, j * 128 : (j + 1) * 128]
            scaled[k, r * answer : (r + 1) * answer] = (x * gain[:, at]).astype(BF)
        partial = jnp.dot(scaled[k], weights[at], preferred_element_type=F32)
        if k == 0:
            product[...] = partial
        elif k < steps - 1:
            product[...] += partial
        else:
            partial = product[...] + partial
            lane = lax.broadcasted_iota(jnp.int32, (answer, 128), 1)
            for r in range(count):
                total = jnp.sum(squares[r], axis=-1, keepdims=True)
                high = total.astype(BF).astype(F32)
                pair = jnp.where(lane == 0, high, jnp.where(lane == 1, total - high, 0.0))
                out = outs[r]
                out[:, : queries + 2 * HD] = partial[r * answer : (r + 1) * answer].astype(BF)
                out[:, queries + 2 * HD :] = pair.astype(BF)


def project(place, hidden, gain, w_query, w_key, w_value):
    count, answer, width = hidden.shape
    total = w_query.shape[1] + 2 * HD
    steps = 4
    smem = pl.BlockSpec(memory_space=pltpu.SMEM)
    vmem = pl.BlockSpec(memory_space=pltpu.VMEM)
    anywhere = pl.BlockSpec(memory_space=pl.ANY)
    return pl.pallas_call(
        project_kernel,
        in_specs=[smem, anywhere, vmem, anywhere, anywhere, anywhere],
        out_specs=[vmem] * count,
        out_shape=[jax.ShapeDtypeStruct((answer, total + HD), BF)] * count,
        scratch_shapes=[
            pltpu.VMEM((steps, count, answer, width // steps), BF),
            pltpu.VMEM((width, total), BF),
            pltpu.VMEM((steps, count * answer, width // steps), BF),
            pltpu.VMEM((count * answer, total), F32),
            pltpu.SemaphoreType.DMA((steps, count + 3)),
        ],
        compiler_params=pltpu.CompilerParams(vmem_limit_bytes=60 * MIB),
        cost_estimate=pl.CostEstimate(
            flops=2 * count * answer * width * total, bytes_accessed=9 * MIB, transcendentals=0
        ),
        name="project",
    )(place, hidden, gain, w_query, w_key, w_value)


def rotate_kernel(place, p0, p1, p2, p3, cosine, sine, cache_key, cache_value, before1, before3,
                  queries, near_key, near_value, piece, sem):
    size = piece.shape[1]
    at = pl.ds(pl.multiple_of(place[1] * size, size), size)
    copies = [
        pltpu.make_async_copy(cache.at[at], piece.at[i], sem.at[i])
        for i, cache in enumerate((cache_key, cache_value))
    ]
    for copy in copies:
        copy.start()
    answer = p0.shape[0]
    span = answer // HALVES
    heads = queries.shape[0] // answer
    width = (heads + 2) * HD
    total = (
        p0[:, width:].astype(F32) + p1[:, width:].astype(F32)
        + p2[:, width:].astype(F32) + p3[:, width:].astype(F32)
    )
    scale = lax.rsqrt((total[:, 0:1] + total[:, 1:2]) / D + norm_eps)

    def column(h):
        at = slice(h * HD, (h + 1) * HD)
        return (
            p0[:, at].astype(F32) + p1[:, at].astype(F32)
            + p2[:, at].astype(F32) + p3[:, at].astype(F32)
        ) * scale

    def turned(x):
        return x * cosine[...] + pltpu.roll(x, HD // 2, 1) * sine[...]

    factor = math.log2(math.e) / math.sqrt(HD)
    for n in range(heads):
        q = (turned(column(n)) * factor).astype(BF)
        for h in range(HALVES):
            start = (h * heads + n) * span
            queries[start : start + span] = q[h * span : (h + 1) * span]
    near_key[...] = turned(column(heads)).astype(BF)
    near_value[...] = column(heads + 1).astype(BF)
    for copy in copies:
        copy.wait()


def rotate(place, parts, cosine, sine, cache_key, cache_value, before):
    answer = parts[0].shape[0]
    heads = parts[0].shape[1] // HD - 3
    vmem = pl.BlockSpec(memory_space=pltpu.VMEM)
    anywhere = pl.BlockSpec(memory_space=pl.ANY)
    return pl.pallas_call(
        rotate_kernel,
        in_specs=[pl.BlockSpec(memory_space=pltpu.SMEM)] + [vmem] * 6 + [anywhere] * 4,
        out_specs=[vmem] * 3 + [anywhere],
        out_shape=[
            jax.ShapeDtypeStruct((heads * answer, HD), BF),
            jax.ShapeDtypeStruct((answer, HD), BF),
            jax.ShapeDtypeStruct((answer, HD), BF),
            jax.ShapeDtypeStruct((2, cache_key.shape[0] // 2, HD), BF),
        ],
        scratch_shapes=[pltpu.SemaphoreType.DMA((2,))],
        compiler_params=pltpu.CompilerParams(vmem_limit_bytes=16 * MIB),
        cost_estimate=pl.CostEstimate(
            flops=20 * answer * heads * HD, bytes_accessed=3 * MIB, transcendentals=0
        ),
        name="rotate",
    )(place, *parts, cosine, sine, cache_key, cache_value, *before)


def ones_column(rows):
    return jnp.where(lax.broadcasted_iota(jnp.int32, (rows, HD), 1) == 0, 1.0, 0.0).astype(BF)


def fill_section(mask, section, source, slot, local, keys, values):
    ones = ones_column(BLOCK)
    blocks = local // BLOCK

    def fill(b, carry):
        at = pl.ds(pl.multiple_of(slot * local + b * BLOCK, BLOCK), BLOCK)
        bias = jnp.where(mask[section, source * blocks + b] > 0, 0.0, masked_score)
        keys[at, HD:] = jnp.full((BLOCK, HD), bias, F32).astype(BF)
        values[at, HD:] = ones
        return carry

    lax.fori_loop(0, blocks, fill, 0, unroll=4)


def sweep(q_aug, keys, values, buffers, m, acc):
    tile = buffers[0].shape[1]
    tiles = keys.shape[0] // tile
    dims = (((1,), (1,)), ((), ()))

    def score(t):
        s = lax.dot_general(
            q_aug, keys[t * tile : (t + 1) * tile], dims, preferred_element_type=F32
        )
        buffers[t % 2][...] = s
        return jnp.max(s, axis=-1, keepdims=True)

    top = score(0)
    for t in range(tiles):
        m_new = jnp.maximum(m, top)
        if t + 1 < tiles:
            top = score(t + 1)
        p = jnp.exp2(buffers[t % 2][...] - m_new).astype(BF)
        acc = acc * jnp.exp2(m - m_new) + jnp.dot(
            p, values[t * tile : (t + 1) * tile], preferred_element_type=F32
        )
        m = m_new
    return m, acc


def near_kernel(place, mask, queries, near_key, near_value, own_key, own_value, a1, b1, a3, b3,
                out, keys, values, near_values, buf0, buf1, sem):
    section, core = place[0], place[1]
    answer = near_key.shape[0]
    span = answer // HALVES
    rows = queries.shape[0] // HALVES
    local = own_key.shape[0]
    size = local // 2
    sections = mask.shape[1] * BLOCK // local

    copies = []

    def bring(source, buffer, start, size):
        copy = pltpu.make_async_copy(
            source,
            buffer.at[pl.ds(pl.multiple_of(start, size), size), pl.ds(0, HD)],
            sem.at[len(copies)],
        )
        copy.start()
        copies.append(copy)

    bring(own_key, keys, 0, local)
    bring(own_value, values, 0, local)
    for slot, pieces in ((1, (a1, b1)), (2, (a3, b3))):
        for piece, side in zip(pieces, (core, 1 - core)):
            for kind, buffer in ((0, keys), (1, values)):
                bring(piece.at[kind], buffer, slot * local + side * size, size)
    for slot, source in enumerate((section, section + sections - 1, section + 1)):
        fill_section(mask, section, lax.rem(source, sections), slot, local, keys, values)
    near_values[:, :HD] = near_value[...]
    near_values[:, HD:] = ones_column(answer)
    for copy in copies:
        copy.wait()

    ones = ones_column(rows)
    dims = (((1,), (1,)), ((), ()))
    row = lax.rem(lax.broadcasted_iota(jnp.int32, (rows, answer), 0), span)
    column = lax.broadcasted_iota(jnp.int32, (rows, answer), 1)
    lane = lax.broadcasted_iota(jnp.int32, (rows, HD), 1)

    def half(h, carry):
        at = pl.ds(pl.multiple_of(h * rows, rows), rows)
        q = queries[at]
        s = lax.dot_general(q, near_key[...], dims, preferred_element_type=F32)
        s = jnp.where(row + h * span >= column, s, masked_score)
        m = jnp.max(s, axis=-1, keepdims=True)
        acc = jnp.dot(jnp.exp2(s - m).astype(BF), near_values[...], preferred_element_type=F32)
        m, acc = sweep(jnp.concatenate([q, ones], axis=1), keys, values, (buf0, buf1), m, acc)
        out[at, :HD] = acc[:, :HD]
        out[at, HD:] = jnp.where(lane == 1, m, acc[:, HD:])
        return carry

    lax.fori_loop(0, HALVES, half, 0)


def attend_near(place, mask, queries, near_key, near_value, own_key, own_value, pieces):
    rows = queries.shape[0]
    answer = near_key.shape[0]
    context = 3 * own_key.shape[0]
    vmem = pl.BlockSpec(memory_space=pltpu.VMEM)
    smem = pl.BlockSpec(memory_space=pltpu.SMEM)
    anywhere = pl.BlockSpec(memory_space=pl.ANY)
    return pl.pallas_call(
        near_kernel,
        in_specs=[smem, smem] + [vmem] * 3 + [anywhere] * 6,
        out_specs=vmem,
        out_shape=jax.ShapeDtypeStruct((rows, 2 * HD), F32),
        scratch_shapes=[
            pltpu.VMEM((context, 2 * HD), BF),
            pltpu.VMEM((context, 2 * HD), BF),
            pltpu.VMEM((answer, 2 * HD), BF),
            pltpu.VMEM((rows // HALVES, TILE), F32),
            pltpu.VMEM((rows // HALVES, TILE), F32),
            pltpu.SemaphoreType.DMA((10,)),
        ],
        compiler_params=pltpu.CompilerParams(vmem_limit_bytes=32 * MIB),
        cost_estimate=pl.CostEstimate(
            flops=8 * rows * context * HD,
            bytes_accessed=6 * MIB,
            transcendentals=rows * context,
        ),
        name="attend_near",
    )(place, mask, queries, near_key, near_value, own_key, own_value, *pieces)


def far_kernel(place, mask, queries, state, a2, b2, out, keys, values, buf0, buf1, sem):
    section, core = place[0], place[1]
    size = a2.shape[1]
    sections = mask.shape[1] * BLOCK // (2 * size)
    copies = []
    for piece, side in ((a2, core), (b2, 1 - core)):
        for kind, buffer in ((0, keys), (1, values)):
            at = pl.ds(pl.multiple_of(side * size, size), size)
            copies.append(
                pltpu.make_async_copy(
                    piece.at[kind], buffer.at[at, pl.ds(0, HD)], sem.at[len(copies)]
                )
            )
            copies[-1].start()
    source = lax.rem(section + sections - 2, sections)
    fill_section(mask, section, source, 0, 2 * size, keys, values)
    for copy in copies:
        copy.wait()
    rows = queries.shape[0]
    span = out.shape[0]
    q_aug = jnp.concatenate([queries[...], ones_column(rows)], axis=1)
    _, acc = sweep(
        q_aug, keys, values, (buf0, buf1), state[:, HD + 1 : HD + 2], state[...]
    )
    result = (acc[:, :HD] / acc[:, HD : HD + 1]).astype(BF)
    for h in range(rows // span):
        out[:, h * HD : (h + 1) * HD] = result[h * span : (h + 1) * span]


def attend_far(half, place, mask, queries, state, pieces):
    rows = queries.shape[0] // HALVES
    context = 2 * pieces[0].shape[1]
    smem = pl.BlockSpec(memory_space=pltpu.SMEM)
    anywhere = pl.BlockSpec(memory_space=pl.ANY)
    span = ANSWER // HALVES
    return pl.pallas_call(
        far_kernel,
        grid=(1,),
        in_specs=[
            smem,
            smem,
            pl.BlockSpec((rows, HD), lambda i: (half, 0)),
            pl.BlockSpec((rows, 2 * HD), lambda i: (half, 0)),
            anywhere,
            anywhere,
        ],
        out_specs=pl.BlockSpec((span, rows // span * HD), lambda i: (0, 0)),
        out_shape=jax.ShapeDtypeStruct((span, rows // span * HD), BF),
        scratch_shapes=[
            pltpu.VMEM((context, 2 * HD), BF),
            pltpu.VMEM((context, 2 * HD), BF),
            pltpu.VMEM((rows, TILE), F32),
            pltpu.VMEM((rows, TILE), F32),
            pltpu.SemaphoreType.DMA((4,)),
        ],
        compiler_params=pltpu.CompilerParams(vmem_limit_bytes=24 * MIB),
        cost_estimate=pl.CostEstimate(
            flops=8 * rows * context * HD,
            bytes_accessed=3 * MIB,
            transcendentals=rows * context,
        ),
        name="attend_far",
    )(place, mask, queries, state, *pieces)


def output_kernel(place, a0, a1, a2, a3, w_out, before, o0, o1, o2, o3, after, rows, weights, sem):
    count, span, depth = rows.shape
    outs = (o0, o1, o2, o3)
    after[...] = jnp.zeros_like(after)
    width = w_out.shape[1] // len(outs)
    copies = []
    for k in range(len(outs)):
        at = pl.ds(pl.multiple_of(lax.rem(place[2] + k, len(outs)) * width, width), width)
        copies.append(pltpu.make_async_copy(w_out.at[:, at], weights.at[k], sem.at[k]))
        copies[-1].start()
    for r, part in enumerate((a0, a1, a2, a3)):
        rows[lax.rem(place[0] + count - r, count)] = part[...]
    left = rows[...].reshape(count * span, depth)
    for k, out in enumerate(outs):
        copies[k].wait()
        for side in range(2):
            at = slice(side * width // 2, (side + 1) * width // 2)
            out[side] = jnp.dot(left, weights[k, :, at], preferred_element_type=F32).astype(
                out.dtype
            )


def project_out(place, parts, w_out, before):
    span, depth = parts[0].shape
    count = len(parts)
    width = w_out.shape[1] // 4
    vmem = pl.BlockSpec(memory_space=pltpu.VMEM)
    smem = pl.BlockSpec(memory_space=pltpu.SMEM)
    shape = (2, count * span, width // 2)
    return pl.pallas_call(
        output_kernel,
        in_specs=[smem] + [vmem] * count + [pl.BlockSpec(memory_space=pl.ANY)] * 2,
        out_specs=[vmem] * 5,
        out_shape=[jax.ShapeDtypeStruct(shape, F32)]
        + [jax.ShapeDtypeStruct(shape, BF)] * 3
        + [jax.ShapeDtypeStruct((8, 128), F32)],
        scratch_shapes=[
            pltpu.VMEM((count, span, depth), BF),
            pltpu.VMEM((4, depth, width), BF),
            pltpu.SemaphoreType.DMA((4,)),
        ],
        compiler_params=pltpu.CompilerParams(vmem_limit_bytes=24 * MIB),
        cost_estimate=pl.CostEstimate(
            flops=8 * count * span * depth * width, bytes_accessed=6 * MIB, transcendentals=0
        ),
        name="project_out",
    )(place, *parts, w_out, before)


def reduce_kernel(half, place, *refs):
    earlier, pieces, (send, keep) = refs[: 2 * half], refs[2 * half : -2], refs[-2:]
    count, rows, _ = keep.shape
    span = rows // (half + 1)
    for done, out in zip(earlier, (send, keep)):
        out[:, : half * span] = done[...]
    for side, out in ((1 - place[3], send), (place[3], keep)):
        total = pieces[0][side].astype(F32)
        for piece in pieces[1:]:
            total = total + piece[side].astype(F32)
        for c in range(count):
            out[c, half * span :] = total[c * span : (c + 1) * span].astype(out.dtype)


def reduce_pieces(half, place, earlier, pieces, count):
    _, rows, width = pieces[0].shape
    shape = (count, rows // count * (half + 1), width)
    vmem = pl.BlockSpec(memory_space=pltpu.VMEM)
    return pl.pallas_call(
        functools.partial(reduce_kernel, half),
        in_specs=[pl.BlockSpec(memory_space=pltpu.SMEM)] + [vmem] * len((*earlier, *pieces)),
        out_specs=[vmem] * 2,
        out_shape=[jax.ShapeDtypeStruct(shape, BF), jax.ShapeDtypeStruct(shape, F32)],
        compiler_params=pltpu.CompilerParams(vmem_limit_bytes=16 * MIB),
        cost_estimate=pl.CostEstimate(
            flops=8 * rows * width, bytes_accessed=16 * rows * width, transcendentals=0
        ),
        name="reduce_pieces",
    )(place, *earlier, *pieces)


def rotation(answer):
    half = HD // 2
    positions = (NBLK * BLOCK + jnp.arange(answer)).astype(F32)
    frequency = rope_base ** (-2.0 * jnp.arange(half).astype(F32) / HD)
    angles = positions[:, None] * frequency[None, :]
    cosine, sine = jnp.cos(angles), jnp.sin(angles)
    return jnp.concatenate([cosine, cosine], axis=1), jnp.concatenate([-sine, sine], axis=1)


def per_device(
    hidden, norm_gain, w_query, w_key, w_value, w_out, cache_key, cache_value, block_mask
):
    section = lax.axis_index("section")
    core = lax.rem(lax.axis_index("coal"), 2)
    tensor = lax.axis_index("tensor")
    z_hi = lax.rem(tensor, 2)
    place = jnp.stack([section, core, tensor // 2, z_hi]).astype(jnp.int32)
    answer = hidden.shape[1]
    half_rows = cache_key.shape[0] // 2
    piece = jnp.stack(
        [
            lax.dynamic_slice_in_dim(cache_key, core * half_rows, half_rows, 0),
            lax.dynamic_slice_in_dim(cache_value, core * half_rows, half_rows, 0),
        ]
    )
    with jax.named_scope("cache"):
        mine = {r: section_shift(piece, r) for r in (1, 3)}
    with jax.named_scope("swap"):
        other = {r: core_swap(mine[r]) for r in (1, 3)}
    cosine, sine = rotation(answer)

    chunks = project(place, hidden, norm_gain[None, :], w_query, w_key, w_value)
    with jax.named_scope("sums"):
        parts = [chunks[0]] + [section_shift(chunks[r], r) for r in (1, 3, 2)]
    queries, near_key, near_value, piece = rotate(
        place, parts, cosine, sine, cache_key, cache_value, (other[1], other[3])
    )
    with jax.named_scope("cache2"):
        mine[2] = section_shift(piece, 2)
    state = attend_near(
        place, block_mask, queries, near_key, near_value, cache_key, cache_value,
        (mine[1], other[1], mine[3], other[3]),
    )
    with jax.named_scope("swap2"):
        other[2] = core_swap(mine[2] + (state[0, HD + 1] * 0.0).astype(BF))
    attended, gathered = [], []
    for h in range(HALVES):
        attention = attend_far(h, place, block_mask, queries, state, (mine[2], other[2]))
        attended.append(attention)
        with jax.named_scope(f"gather{h}"):
            gathered.append([attention] + [section_shift(attention, r) for r in (1, 2, 3)])

    reduced, turn = (), attended[-1]
    for h in range(HALVES):
        *sums, turn = project_out(place, gathered[h], w_out, turn)
        with jax.named_scope(f"x{h}"):
            pieces = [sums[0]] + [x_shift(sums[r], r) for r in (1, 2, 3)]
        reduced = reduce_pieces(h, place, reduced, pieces, hidden.shape[0])
    send, keep = reduced
    with jax.named_scope("z"):
        arrived = z_swap(send)
    return (keep + arrived.astype(F32)).astype(BF)


def solution(mesh):
    return jax.shard_map(
        per_device,
        mesh=mesh,
        in_specs=(
            P("coal", None, "section"),
            P("section"),
            P("section", "tensor"),
            P("section", "tensor"),
            P("section", "tensor"),
            P("tensor", "section"),
            P("section", "tensor"),
            P("section", "tensor"),
            P("coal", None),
        ),
        out_specs=P("coal", None, ("section", "tensor")),
        check_vma=False,
    )
```

```python
import functools
import math

import jax
import jax.numpy as jnp
from jax import lax
from jax.experimental import pallas as pl
from jax.experimental.pallas import tpu as pltpu
from jax.sharding import PartitionSpec as P

D = 8192
HD = 128
NBLK = 128
BLOCK = 64
rope_base = 500000.0
norm_eps = 1e-05
masked_score = -1e30
BF = jnp.bfloat16
F32 = jnp.float32
HALVES = 2
TILE = 1024
ANSWER = 128
MIB = 1024 * 1024


def section_shift(x, by):
    n = lax.axis_size("section")
    return lax.ppermute(x, "section", [(i, (i + by) % n) for i in range(n)])


def x_shift(x, by):
    n = lax.axis_size("tensor") // 2
    return lax.ppermute(
        x, "tensor", [(i, ((i // 2 + by) % n) * 2 + i % 2) for i in range(2 * n)]
    )


def z_swap(x):
    return lax.ppermute(x, "tensor", [(i, i ^ 1) for i in range(lax.axis_size("tensor"))])


def z_neighbour_swap(x):
    return lax.ppermute(x, "coal", [(i, i ^ 2) for i in range(lax.axis_size("coal"))])


def core_swap(x):
    return lax.ppermute(x, "coal", [(i, i ^ 1) for i in range(lax.axis_size("coal"))])


def project_kernel(place, hidden, gain, w_query, w_key, w_value, *rest):
    outs, (rows, weights, scaled, product, sem) = rest[:-5], rest[-5:]
    count, answer, width = hidden.shape
    queries = w_query.shape[1]
    steps, _, _, depth = rows.shape
    copies = []
    for k in range(steps):
        at = pl.ds(k * depth, depth)
        group = [
            (hidden.at[lax.rem(place[0] + r, count), :, at], rows.at[k, r]) for r in range(count)
        ]
        group += [
            (w_query.at[at], weights.at[at, pl.ds(0, queries)]),
            (w_key.at[at], weights.at[at, pl.ds(queries, HD)]),
            (w_value.at[at], weights.at[at, pl.ds(queries + HD, HD)]),
        ]
        copies.append(
            [pltpu.make_async_copy(a, b, sem.at[k, i]) for i, (a, b) in enumerate(group)]
        )
        for copy in copies[-1]:
            copy.start()

    squares = [jnp.zeros((answer, 128), F32) for _ in range(count)]
    for k in range(steps):
        at = slice(k * depth, (k + 1) * depth)
        for copy in copies[k]:
            copy.wait()
        for r in range(count):
            x = rows[k, r].astype(F32)
            x2 = x * x
            for j in range(depth // 128):
                squares[r] = squares[r] + x2[:, j * 128 : (j + 1) * 128]
            scaled[k, r * answer : (r + 1) * answer] = (x * gain[:, at]).astype(BF)
        partial = jnp.dot(scaled[k], weights[at], preferred_element_type=F32)
        if k == 0:
            product[...] = partial
        elif k < steps - 1:
            product[...] += partial
        else:
            partial = product[...] + partial
            lane = lax.broadcasted_iota(jnp.int32, (answer, 128), 1)
            for r in range(count):
                total = jnp.sum(squares[r], axis=-1, keepdims=True)
                high = total.astype(BF).astype(F32)
                pair = jnp.where(lane == 0, high, jnp.where(lane == 1, total - high, 0.0))
                out = outs[r]
                out[:, : queries + 2 * HD] = partial[r * answer : (r + 1) * answer].astype(BF)
                out[:, queries + 2 * HD :] = pair.astype(BF)


def project(place, hidden, gain, w_query, w_key, w_value):
    count, answer, width = hidden.shape
    total = w_query.shape[1] + 2 * HD
    steps = 4
    smem = pl.BlockSpec(memory_space=pltpu.SMEM)
    vmem = pl.BlockSpec(memory_space=pltpu.VMEM)
    anywhere = pl.BlockSpec(memory_space=pl.ANY)
    return pl.pallas_call(
        project_kernel,
        in_specs=[smem, anywhere, vmem, anywhere, anywhere, anywhere],
        out_specs=[vmem] * count,
        out_shape=[jax.ShapeDtypeStruct((answer, total + HD), BF)] * count,
        scratch_shapes=[
            pltpu.VMEM((steps, count, answer, width // steps), BF),
            pltpu.VMEM((width, total), BF),
            pltpu.VMEM((steps, count * answer, width // steps), BF),
            pltpu.VMEM((count * answer, total), F32),
            pltpu.SemaphoreType.DMA((steps, count + 3)),
        ],
        compiler_params=pltpu.CompilerParams(vmem_limit_bytes=60 * MIB),
        cost_estimate=pl.CostEstimate(
            flops=2 * count * answer * width * total, bytes_accessed=9 * MIB, transcendentals=0
        ),
        name="project",
    )(place, hidden, gain, w_query, w_key, w_value)


def rotate_kernel(place, p0, p1, p2, p3, cosine, sine, cache_key, cache_value, *rest):
    queries, near_key, near_value, piece, sem = rest[-5:]
    size = piece.shape[1]
    at = pl.ds(pl.multiple_of(place[1] * size, size), size)
    copies = [
        pltpu.make_async_copy(cache.at[at], piece.at[i], sem.at[i])
        for i, cache in enumerate((cache_key, cache_value))
    ]
    for copy in copies:
        copy.start()
    answer = p0.shape[0]
    span = answer // HALVES
    heads = queries.shape[0] // answer
    width = (heads + 2) * HD
    total = (
        p0[:, width:].astype(F32) + p1[:, width:].astype(F32)
        + p2[:, width:].astype(F32) + p3[:, width:].astype(F32)
    )
    scale = lax.rsqrt((total[:, 0:1] + total[:, 1:2]) / D + norm_eps)

    def column(h):
        at = slice(h * HD, (h + 1) * HD)
        return (
            p0[:, at].astype(F32) + p1[:, at].astype(F32)
            + p2[:, at].astype(F32) + p3[:, at].astype(F32)
        ) * scale

    def turned(x):
        return x * cosine[...] + pltpu.roll(x, HD // 2, 1) * sine[...]

    factor = math.log2(math.e) / math.sqrt(HD)
    for n in range(heads):
        q = (turned(column(n)) * factor).astype(BF)
        for h in range(HALVES):
            start = (h * heads + n) * span
            queries[start : start + span] = q[h * span : (h + 1) * span]
    near_key[...] = turned(column(heads)).astype(BF)
    near_value[...] = column(heads + 1).astype(BF)
    for copy in copies:
        copy.wait()


def rotate(place, parts, cosine, sine, cache_key, cache_value, before):
    answer = parts[0].shape[0]
    heads = parts[0].shape[1] // HD - 3
    vmem = pl.BlockSpec(memory_space=pltpu.VMEM)
    anywhere = pl.BlockSpec(memory_space=pl.ANY)
    return pl.pallas_call(
        rotate_kernel,
        in_specs=[pl.BlockSpec(memory_space=pltpu.SMEM)] + [vmem] * 6
        + [anywhere] * (2 + len(before)),
        out_specs=[vmem] * 3 + [anywhere],
        out_shape=[
            jax.ShapeDtypeStruct((heads * answer, HD), BF),
            jax.ShapeDtypeStruct((answer, HD), BF),
            jax.ShapeDtypeStruct((answer, HD), BF),
            jax.ShapeDtypeStruct((2, cache_key.shape[0] // 2, HD), BF),
        ],
        scratch_shapes=[pltpu.SemaphoreType.DMA((2,))],
        compiler_params=pltpu.CompilerParams(vmem_limit_bytes=16 * MIB),
        cost_estimate=pl.CostEstimate(
            flops=20 * answer * heads * HD, bytes_accessed=3 * MIB, transcendentals=0
        ),
        name="rotate",
    )(place, *parts, cosine, sine, cache_key, cache_value, *before)


def ones_column(rows):
    return jnp.where(lax.broadcasted_iota(jnp.int32, (rows, HD), 1) == 0, 1.0, 0.0).astype(BF)


def fill_section(mask, section, source, slot, local, keys, values):
    ones = ones_column(BLOCK)
    blocks = local // BLOCK

    def fill(b, carry):
        at = pl.ds(pl.multiple_of(slot * local + b * BLOCK, BLOCK), BLOCK)
        bias = jnp.where(mask[section, source * blocks + b] > 0, 0.0, masked_score)
        keys[at, HD:] = jnp.full((BLOCK, HD), bias, F32).astype(BF)
        values[at, HD:] = ones
        return carry

    lax.fori_loop(0, blocks, fill, 0, unroll=4)


def sweep(q_aug, keys, values, buffers, m, acc):
    tile = buffers[0].shape[1]
    tiles = keys.shape[0] // tile
    dims = (((1,), (1,)), ((), ()))

    def score(t):
        s = lax.dot_general(
            q_aug, keys[t * tile : (t + 1) * tile], dims, preferred_element_type=F32
        )
        buffers[t % 2][...] = s
        return jnp.max(s, axis=-1, keepdims=True)

    top = score(0)
    for t in range(tiles):
        m_new = jnp.maximum(m, top)
        if t + 1 < tiles:
            top = score(t + 1)
        p = jnp.exp2(buffers[t % 2][...] - m_new).astype(BF)
        acc = acc * jnp.exp2(m - m_new) + jnp.dot(
            p, values[t * tile : (t + 1) * tile], preferred_element_type=F32
        )
        m = m_new
    return m, acc


def near_kernel(place, mask, queries, near_key, near_value, own_key, own_value, *rest):
    quarters, rest = rest[:8], rest[8:]
    out, keys, values, near_values, buf0, buf1, sem = rest
    section, quarter = place[0], place[4]
    answer = near_key.shape[0]
    span = answer // HALVES
    rows = queries.shape[0] // HALVES
    local = own_key.shape[0]
    size = local // 4
    sections = mask.shape[1] * BLOCK // local

    copies = []

    def bring(source, buffer, start, size):
        copy = pltpu.make_async_copy(
            source,
            buffer.at[pl.ds(pl.multiple_of(start, size), size), pl.ds(0, HD)],
            sem.at[len(copies)],
        )
        copy.start()
        copies.append(copy)

    bring(own_key, keys, 0, local)
    bring(own_value, values, 0, local)
    for slot, pieces in ((1, quarters[:4]), (2, quarters[4:])):
        for n, piece in enumerate(pieces):
            side = quarter ^ n
            for kind, buffer in ((0, keys), (1, values)):
                bring(piece.at[kind], buffer, slot * local + side * size, size)
    for slot, source in enumerate((section, section + sections - 1, section + 1)):
        fill_section(mask, section, lax.rem(source, sections), slot, local, keys, values)
    near_values[:, :HD] = near_value[...]
    near_values[:, HD:] = ones_column(answer)
    for copy in copies:
        copy.wait()

    ones = ones_column(rows)
    dims = (((1,), (1,)), ((), ()))
    row = lax.rem(lax.broadcasted_iota(jnp.int32, (rows, answer), 0), span)
    column = lax.broadcasted_iota(jnp.int32, (rows, answer), 1)
    lane = lax.broadcasted_iota(jnp.int32, (rows, HD), 1)

    def half(h, carry):
        at = pl.ds(pl.multiple_of(h * rows, rows), rows)
        q = queries[at]
        s = lax.dot_general(q, near_key[...], dims, preferred_element_type=F32)
        s = jnp.where(row + h * span >= column, s, masked_score)
        m = jnp.max(s, axis=-1, keepdims=True)
        acc = jnp.dot(jnp.exp2(s - m).astype(BF), near_values[...], preferred_element_type=F32)
        m, acc = sweep(jnp.concatenate([q, ones], axis=1), keys, values, (buf0, buf1), m, acc)
        out[at, :HD] = acc[:, :HD]
        out[at, HD:] = jnp.where(lane == 1, m, acc[:, HD:])
        return carry

    lax.fori_loop(0, HALVES, half, 0)


def attend_near(place, mask, queries, near_key, near_value, own_key, own_value, pieces):
    rows = queries.shape[0]
    answer = near_key.shape[0]
    context = 3 * own_key.shape[0]
    vmem = pl.BlockSpec(memory_space=pltpu.VMEM)
    smem = pl.BlockSpec(memory_space=pltpu.SMEM)
    anywhere = pl.BlockSpec(memory_space=pl.ANY)
    return pl.pallas_call(
        near_kernel,
        in_specs=[smem, smem] + [vmem] * 3 + [anywhere] * 10,
        out_specs=vmem,
        out_shape=jax.ShapeDtypeStruct((rows, 2 * HD), F32),
        scratch_shapes=[
            pltpu.VMEM((context, 2 * HD), BF),
            pltpu.VMEM((context, 2 * HD), BF),
            pltpu.VMEM((answer, 2 * HD), BF),
            pltpu.VMEM((rows // HALVES, TILE), F32),
            pltpu.VMEM((rows // HALVES, TILE), F32),
            pltpu.SemaphoreType.DMA((18,)),
        ],
        compiler_params=pltpu.CompilerParams(vmem_limit_bytes=32 * MIB),
        cost_estimate=pl.CostEstimate(
            flops=8 * rows * context * HD,
            bytes_accessed=6 * MIB,
            transcendentals=rows * context,
        ),
        name="attend_near",
    )(place, mask, queries, near_key, near_value, own_key, own_value, *pieces)


def far_kernel(place, mask, queries, state, a2, b2, out, keys, values, buf0, buf1, sem):
    section, core = place[0], place[1]
    size = a2.shape[1]
    sections = mask.shape[1] * BLOCK // (2 * size)
    copies = []
    for piece, side in ((a2, core), (b2, 1 - core)):
        for kind, buffer in ((0, keys), (1, values)):
            at = pl.ds(pl.multiple_of(side * size, size), size)
            copies.append(
                pltpu.make_async_copy(
                    piece.at[kind], buffer.at[at, pl.ds(0, HD)], sem.at[len(copies)]
                )
            )
            copies[-1].start()
    source = lax.rem(section + sections - 2, sections)
    fill_section(mask, section, source, 0, 2 * size, keys, values)
    for copy in copies:
        copy.wait()
    rows = queries.shape[0]
    span = out.shape[0]
    q_aug = jnp.concatenate([queries[...], ones_column(rows)], axis=1)
    _, acc = sweep(
        q_aug, keys, values, (buf0, buf1), state[:, HD + 1 : HD + 2], state[...]
    )
    result = (acc[:, :HD] / acc[:, HD : HD + 1]).astype(BF)
    for h in range(rows // span):
        out[:, h * HD : (h + 1) * HD] = result[h * span : (h + 1) * span]


def attend_far(half, place, mask, queries, state, pieces):
    rows = queries.shape[0] // HALVES
    context = 2 * pieces[0].shape[1]
    smem = pl.BlockSpec(memory_space=pltpu.SMEM)
    anywhere = pl.BlockSpec(memory_space=pl.ANY)
    span = ANSWER // HALVES
    return pl.pallas_call(
        far_kernel,
        grid=(1,),
        in_specs=[
            smem,
            smem,
            pl.BlockSpec((rows, HD), lambda i: (half, 0)),
            pl.BlockSpec((rows, 2 * HD), lambda i: (half, 0)),
            anywhere,
            anywhere,
        ],
        out_specs=pl.BlockSpec((span, rows // span * HD), lambda i: (0, 0)),
        out_shape=jax.ShapeDtypeStruct((span, rows // span * HD), BF),
        scratch_shapes=[
            pltpu.VMEM((context, 2 * HD), BF),
            pltpu.VMEM((context, 2 * HD), BF),
            pltpu.VMEM((rows, TILE), F32),
            pltpu.VMEM((rows, TILE), F32),
            pltpu.SemaphoreType.DMA((4,)),
        ],
        compiler_params=pltpu.CompilerParams(vmem_limit_bytes=24 * MIB),
        cost_estimate=pl.CostEstimate(
            flops=8 * rows * context * HD,
            bytes_accessed=3 * MIB,
            transcendentals=rows * context,
        ),
        name="attend_far",
    )(place, mask, queries, state, *pieces)


def output_kernel(place, a0, a1, a2, a3, w_out, before, o0, o1, o2, o3, after, rows, weights, sem):
    count, span, depth = rows.shape
    outs = (o0, o1, o2, o3)
    after[...] = jnp.zeros_like(after)
    width = w_out.shape[1] // len(outs)
    copies = []
    for k in range(len(outs)):
        at = pl.ds(pl.multiple_of(lax.rem(place[2] + k, len(outs)) * width, width), width)
        copies.append(pltpu.make_async_copy(w_out.at[:, at], weights.at[k], sem.at[k]))
        copies[-1].start()
    for r, part in enumerate((a0, a1, a2, a3)):
        rows[lax.rem(place[0] + count - r, count)] = part[...]
    left = rows[...].reshape(count * span, depth)
    for k, out in enumerate(outs):
        copies[k].wait()
        for side in range(2):
            at = slice(side * width // 2, (side + 1) * width // 2)
            out[side] = jnp.dot(left, weights[k, :, at], preferred_element_type=F32).astype(
                out.dtype
            )


def project_out(place, parts, w_out, before):
    span, depth = parts[0].shape
    count = len(parts)
    width = w_out.shape[1] // 4
    vmem = pl.BlockSpec(memory_space=pltpu.VMEM)
    smem = pl.BlockSpec(memory_space=pltpu.SMEM)
    shape = (2, count * span, width // 2)
    return pl.pallas_call(
        output_kernel,
        in_specs=[smem] + [vmem] * count + [pl.BlockSpec(memory_space=pl.ANY)] * 2,
        out_specs=[vmem] * 5,
        out_shape=[jax.ShapeDtypeStruct(shape, F32)]
        + [jax.ShapeDtypeStruct(shape, BF)] * 3
        + [jax.ShapeDtypeStruct((8, 128), F32)],
        scratch_shapes=[
            pltpu.VMEM((count, span, depth), BF),
            pltpu.VMEM((4, depth, width), BF),
            pltpu.SemaphoreType.DMA((4,)),
        ],
        compiler_params=pltpu.CompilerParams(vmem_limit_bytes=24 * MIB),
        cost_estimate=pl.CostEstimate(
            flops=8 * count * span * depth * width, bytes_accessed=6 * MIB, transcendentals=0
        ),
        name="project_out",
    )(place, *parts, w_out, before)


def reduce_kernel(place, before, *refs):
    pieces, (send, keep) = refs[:-2], refs[-2:]
    for side, out in ((1 - place[3], send), (place[3], keep)):
        total = pieces[0][side].astype(F32)
        for piece in pieces[1:]:
            total = total + piece[side].astype(F32)
        out[...] = total.astype(out.dtype)


def reduce_pieces(place, before, pieces):
    _, rows, width = pieces[0].shape
    vmem = pl.BlockSpec(memory_space=pltpu.VMEM)
    return pl.pallas_call(
        reduce_kernel,
        in_specs=[pl.BlockSpec(memory_space=pltpu.SMEM), pl.BlockSpec(memory_space=pl.ANY)]
        + [vmem] * len(pieces),
        out_specs=[vmem] * 2,
        out_shape=[jax.ShapeDtypeStruct((rows, width), t) for t in (BF, F32)],
        compiler_params=pltpu.CompilerParams(vmem_limit_bytes=16 * MIB),
        cost_estimate=pl.CostEstimate(flops=8 * rows * width, bytes_accessed=16 * rows * width, transcendentals=0),
        name="reduce_pieces",
    )(place, before, *pieces)


def rotation(answer):
    half = HD // 2
    positions = (NBLK * BLOCK + jnp.arange(answer)).astype(F32)
    frequency = rope_base ** (-2.0 * jnp.arange(half).astype(F32) / HD)
    angles = positions[:, None] * frequency[None, :]
    cosine, sine = jnp.cos(angles), jnp.sin(angles)
    return jnp.concatenate([cosine, cosine], axis=1), jnp.concatenate([-sine, sine], axis=1)


def per_device(
    hidden, norm_gain, w_query, w_key, w_value, w_out, cache_key, cache_value, block_mask
):
    section = lax.axis_index("section")
    core = lax.rem(lax.axis_index("coal"), 2)
    tensor = lax.axis_index("tensor")
    z_hi = lax.rem(tensor, 2)
    quarter = lax.rem(lax.axis_index("coal"), 4)
    place = jnp.stack([section, core, tensor // 2, z_hi, quarter]).astype(jnp.int32)
    answer = hidden.shape[1]
    quarter_rows = cache_key.shape[0] // 4
    piece = jnp.stack(
        [
            lax.dynamic_slice_in_dim(cache_key, quarter * quarter_rows, quarter_rows, 0),
            lax.dynamic_slice_in_dim(cache_value, quarter * quarter_rows, quarter_rows, 0),
        ]
    )
    with jax.named_scope("cache"):
        mine = {r: section_shift(piece, r) for r in (1, 3)}
    quarters = []
    for r in (1, 3):
        with jax.named_scope("swap"):
            beside = core_swap(mine[r])
        with jax.named_scope("zcache"):
            over = z_neighbour_swap(mine[r])
        with jax.named_scope("zswap"):
            both = core_swap(over)
        quarters += [mine[r], beside, over, both]
    cosine, sine = rotation(answer)

    chunks = project(place, hidden, norm_gain[None, :], w_query, w_key, w_value)
    with jax.named_scope("sums"):
        parts = [chunks[0]] + [section_shift(chunks[r], r) for r in (1, 3, 2)]
    queries, near_key, near_value, piece = rotate(
        place, parts, cosine, sine, cache_key, cache_value, quarters
    )
    with jax.named_scope("cache2"):
        far_mine = section_shift(piece, 2)
    state = attend_near(
        place, block_mask, queries, near_key, near_value, cache_key, cache_value,
        quarters,
    )
    with jax.named_scope("swap2"):
        far_other = core_swap(far_mine + (state[0, HD + 1] * 0.0).astype(BF))
    attended, gathered = [], []
    for h in range(HALVES):
        attention = attend_far(h, place, block_mask, queries, state, (far_mine, far_other))
        attended.append(attention)
        with jax.named_scope(f"gather{h}"):
            gathered.append([attention] + [section_shift(attention, r) for r in (1, 2, 3)])

    turn, send, results = attended[-1], queries, []
    for h in range(HALVES):
        *sums, turn = project_out(place, gathered[h], w_out, turn)
        with jax.named_scope(f"x{h}"):
            pieces = [sums[0]] + [x_shift(sums[r], r) for r in (1, 2, 3)]
        send, keep = reduce_pieces(place, send, pieces)
        with jax.named_scope(f"z{h}"):
            arrived = z_swap(send)
        result = (keep + arrived.astype(F32)).astype(BF)
        results.append(result.reshape(hidden.shape[0], answer // HALVES, -1))
    return jnp.concatenate(results, axis=1)


def solution(mesh):
    return jax.shard_map(
        per_device,
        mesh=mesh,
        in_specs=(
            P("coal", None, "section"),
            P("section"),
            P("section", "tensor"),
            P("section", "tensor"),
            P("section", "tensor"),
            P("tensor", "section"),
            P("section", "tensor"),
            P("section", "tensor"),
            P("coal", None),
        ),
        out_specs=P("coal", None, ("section", "tensor")),
        check_vma=False,
    )
```

```python
import functools
import math

import jax
import jax.numpy as jnp
from jax import lax
from jax.experimental import pallas as pl
from jax.experimental.pallas import tpu as pltpu
from jax.sharding import PartitionSpec as P

D = 8192
HD = 128
NBLK = 128
BLOCK = 64
rope_base = 500000.0
norm_eps = 1e-05
masked_score = -1e30
BF = jnp.bfloat16
F32 = jnp.float32
HALVES = 2
TILE = 1024
LOOPS = 2
MIB = 1024 * 1024


def section_shift(x, by):
    n = lax.axis_size("section")
    return lax.ppermute(x, "section", [(i, (i + by) % n) for i in range(n)])


def x_shift(x, by):
    n = lax.axis_size("tensor") // 2
    return lax.ppermute(
        x, "tensor", [(i, ((i // 2 + by) % n) * 2 + i % 2) for i in range(2 * n)]
    )


def z_swap(x):
    return lax.ppermute(x, "tensor", [(i, i ^ 1) for i in range(lax.axis_size("tensor"))])


def z_neighbour_swap(x):
    return lax.ppermute(x, "coal", [(i, i ^ 2) for i in range(lax.axis_size("coal"))])


def core_swap(x):
    return lax.ppermute(x, "coal", [(i, i ^ 1) for i in range(lax.axis_size("coal"))])


def project_kernel(place, hidden, gain, w_query, w_key, w_value, *rest):
    outs, (rows, weights, scaled, product, sem) = rest[:-5], rest[-5:]
    count, answer, width = hidden.shape
    queries = w_query.shape[1]
    steps, _, _, depth = rows.shape
    copies = []
    for k in range(steps):
        at = pl.ds(k * depth, depth)
        group = [
            (hidden.at[lax.rem(place[0] + r, count), :, at], rows.at[k, r]) for r in range(count)
        ]
        group += [
            (w_query.at[at], weights.at[at, pl.ds(0, queries)]),
            (w_key.at[at], weights.at[at, pl.ds(queries, HD)]),
            (w_value.at[at], weights.at[at, pl.ds(queries + HD, HD)]),
        ]
        copies.append(
            [pltpu.make_async_copy(a, b, sem.at[k, i]) for i, (a, b) in enumerate(group)]
        )
        for copy in copies[-1]:
            copy.start()

    squares = [jnp.zeros((answer, 128), F32) for _ in range(count)]
    for k in range(steps):
        at = slice(k * depth, (k + 1) * depth)
        for copy in copies[k]:
            copy.wait()
        for r in range(count):
            x = rows[k, r].astype(F32)
            x2 = x * x
            for j in range(depth // 128):
                squares[r] = squares[r] + x2[:, j * 128 : (j + 1) * 128]
            scaled[k, r * answer : (r + 1) * answer] = (x * gain[:, at]).astype(BF)
        partial = jnp.dot(scaled[k], weights[at], preferred_element_type=F32)
        if k == 0:
            product[...] = partial
        elif k < steps - 1:
            product[...] += partial
        else:
            partial = product[...] + partial
            lane = lax.broadcasted_iota(jnp.int32, (answer, 128), 1)
            for r in range(count):
                total = jnp.sum(squares[r], axis=-1, keepdims=True)
                high = total.astype(BF).astype(F32)
                pair = jnp.where(lane == 0, high, jnp.where(lane == 1, total - high, 0.0))
                out = outs[r]
                out[:, : queries + 2 * HD] = partial[r * answer : (r + 1) * answer].astype(BF)
                out[:, queries + 2 * HD :] = pair.astype(BF)


def project(place, hidden, gain, w_query, w_key, w_value):
    count, answer, width = hidden.shape
    total = w_query.shape[1] + 2 * HD
    steps = 4
    smem = pl.BlockSpec(memory_space=pltpu.SMEM)
    vmem = pl.BlockSpec(memory_space=pltpu.VMEM)
    anywhere = pl.BlockSpec(memory_space=pl.ANY)
    return pl.pallas_call(
        project_kernel,
        in_specs=[smem, anywhere, vmem, anywhere, anywhere, anywhere],
        out_specs=[vmem] * count,
        out_shape=[jax.ShapeDtypeStruct((answer, total + HD), BF)] * count,
        scratch_shapes=[
            pltpu.VMEM((steps, count, answer, width // steps), BF),
            pltpu.VMEM((width, total), BF),
            pltpu.VMEM((steps, count * answer, width // steps), BF),
            pltpu.VMEM((count * answer, total), F32),
            pltpu.SemaphoreType.DMA((steps, count + 3)),
        ],
        compiler_params=pltpu.CompilerParams(vmem_limit_bytes=60 * MIB),
        cost_estimate=pl.CostEstimate(
            flops=2 * count * answer * width * total, bytes_accessed=9 * MIB, transcendentals=0
        ),
        name="project",
    )(place, hidden, gain, w_query, w_key, w_value)


def rotate_kernel(p0, p1, p2, p3, cosine, sine, queries, near_key, near_value):
    answer = p0.shape[0]
    span = answer // HALVES
    heads = queries.shape[0] // answer
    width = (heads + 2) * HD
    total = (
        p0[:, width:].astype(F32) + p1[:, width:].astype(F32)
        + p2[:, width:].astype(F32) + p3[:, width:].astype(F32)
    )
    scale = lax.rsqrt((total[:, 0:1] + total[:, 1:2]) / D + norm_eps)

    def column(h):
        at = slice(h * HD, (h + 1) * HD)
        return (
            p0[:, at].astype(F32) + p1[:, at].astype(F32)
            + p2[:, at].astype(F32) + p3[:, at].astype(F32)
        ) * scale

    def turned(x):
        return x * cosine[...] + pltpu.roll(x, HD // 2, 1) * sine[...]

    factor = math.log2(math.e) / math.sqrt(HD)
    for n in range(heads):
        q = (turned(column(n)) * factor).astype(BF)
        for h in range(HALVES):
            start = (h * heads + n) * span
            queries[start : start + span] = q[h * span : (h + 1) * span]
    near_key[...] = turned(column(heads)).astype(BF)
    near_value[...] = column(heads + 1).astype(BF)


def rotate(parts, cosine, sine):
    answer = parts[0].shape[0]
    heads = parts[0].shape[1] // HD - 3
    vmem = pl.BlockSpec(memory_space=pltpu.VMEM)
    return pl.pallas_call(
        rotate_kernel,
        in_specs=[vmem] * 6,
        out_specs=[vmem] * 3,
        out_shape=[
            jax.ShapeDtypeStruct((heads * answer, HD), BF),
            jax.ShapeDtypeStruct((answer, HD), BF),
            jax.ShapeDtypeStruct((answer, HD), BF),
        ],
        compiler_params=pltpu.CompilerParams(vmem_limit_bytes=16 * MIB),
        cost_estimate=pl.CostEstimate(
            flops=20 * answer * heads * HD, bytes_accessed=3 * MIB, transcendentals=0
        ),
        name="rotate",
    )(*parts, cosine, sine)


def ones_column(rows):
    return jnp.where(lax.broadcasted_iota(jnp.int32, (rows, HD), 1) == 0, 1.0, 0.0).astype(BF)


def attention_kernel(half, place, mask, queries, near_key, near_value, own_key, own_value, *rest):
    pieces, rest = rest[:12], rest[12:]
    out, keys, values, near_values, buf0, buf1, sem = rest
    buffers = (buf0, buf1)
    section, quarter = place[0], place[4]
    answer = near_key.shape[0]
    rows = queries.shape[0]
    span = out.shape[0]
    local = own_key.shape[0]
    size = local // 4
    sections = keys.shape[0] // local

    copies = []

    def bring(source, buffer, start, size):
        copy = pltpu.make_async_copy(
            source,
            buffer.at[pl.ds(pl.multiple_of(start, size), size), pl.ds(0, HD)],
            sem.at[len(copies)],
        )
        copy.start()
        copies.append(copy)

    bring(own_key, keys, section * local, local)
    bring(own_value, values, section * local, local)
    for n, piece in enumerate(pieces):
        source = lax.rem(section + sections - n // 4 - 1, sections)
        for kind, buffer in ((0, keys), (1, values)):
            bring(piece.at[kind], buffer, source * local + (quarter ^ (n % 4)) * size, size)

    ones = ones_column(rows)

    def fill(b, carry):
        at = pl.ds(pl.multiple_of(b * BLOCK, BLOCK), BLOCK)
        bias = jnp.where(mask[section, b] > 0, 0.0, masked_score)
        keys[at, HD:] = jnp.full((BLOCK, HD), bias, F32).astype(BF)
        values[at, HD:] = ones[:BLOCK]
        return carry

    lax.fori_loop(0, keys.shape[0] // BLOCK, fill, 0, unroll=4)
    near_values[:, :HD] = near_value[...]
    near_values[:, HD:] = ones[:answer]

    dims = (((1,), (1,)), ((), ()))
    row = lax.rem(lax.broadcasted_iota(jnp.int32, (rows, answer), 0), span)
    column = lax.broadcasted_iota(jnp.int32, (rows, answer), 1)
    q = queries[...]
    q_aug = jnp.concatenate([q, ones], axis=1)
    s = lax.dot_general(q, near_key[...], dims, preferred_element_type=F32)
    s = jnp.where(row + half * span >= column, s, masked_score)
    m = jnp.max(s, axis=-1, keepdims=True)
    acc = jnp.dot(jnp.exp2(s - m).astype(BF), near_values[...], preferred_element_type=F32)

    for copy in copies:
        copy.wait()

    tile = buf0.shape[1]
    tiles = keys.shape[0] // tile
    each = tiles // LOOPS

    def at(t):
        return pl.ds(pl.multiple_of(t * tile, tile), tile)

    def sweep(i, state):
        m, acc = state

        def score(t):
            s = lax.dot_general(
                q_aug, keys[at(i * each + t)], dims, preferred_element_type=F32
            )
            buffers[t % 2][...] = s
            return jnp.max(s, axis=-1, keepdims=True)

        top = score(0)
        for t in range(each):
            m_new = jnp.maximum(m, top)
            if t + 1 < each:
                top = score(t + 1)
            p = jnp.exp2(buffers[t % 2][...] - m_new).astype(BF)
            acc = acc * jnp.exp2(m - m_new) + jnp.dot(
                p, values[at(i * each + t)], preferred_element_type=F32
            )
            m = m_new
        return m, acc

    m, acc = lax.fori_loop(0, LOOPS, sweep, (m, acc))
    result = (acc[:, :HD] / acc[:, HD : HD + 1]).astype(BF)
    for h in range(rows // span):
        out[:, h * HD : (h + 1) * HD] = result[h * span : (h + 1) * span]


def attend(half, place, mask, queries, near_key, near_value, own_key, own_value, pieces):
    rows = queries.shape[0] // HALVES
    answer = near_key.shape[0]
    span = answer // HALVES
    context = NBLK * BLOCK
    smem = pl.BlockSpec(memory_space=pltpu.SMEM)
    anywhere = pl.BlockSpec(memory_space=pl.ANY)
    whole = pl.BlockSpec((answer, HD), lambda i: (0, 0))
    return pl.pallas_call(
        functools.partial(attention_kernel, half),
        grid=(1,),
        in_specs=[smem, smem, pl.BlockSpec((rows, HD), lambda i: (half, 0)), whole, whole]
        + [anywhere] * (2 + len(pieces)),
        out_specs=pl.BlockSpec((span, rows // span * HD), lambda i: (0, 0)),
        out_shape=jax.ShapeDtypeStruct((span, rows // span * HD), BF),
        scratch_shapes=[
            pltpu.VMEM((context, 2 * HD), BF),
            pltpu.VMEM((context, 2 * HD), BF),
            pltpu.VMEM((answer, 2 * HD), BF),
            pltpu.VMEM((rows, TILE), F32),
            pltpu.VMEM((rows, TILE), F32),
            pltpu.SemaphoreType.DMA((26,)),
        ],
        compiler_params=pltpu.CompilerParams(vmem_limit_bytes=32 * MIB),
        cost_estimate=pl.CostEstimate(
            flops=8 * rows * context * HD,
            bytes_accessed=6 * MIB,
            transcendentals=rows * context,
        ),
        name="attend",
    )(place, mask, queries, near_key, near_value, own_key, own_value, *pieces)


def output_kernel(place, a0, a1, a2, a3, w_out, before, o0, o1, o2, o3, after, rows, weights, sem):
    count, span, depth = rows.shape
    outs = (o0, o1, o2, o3)
    after[...] = jnp.zeros_like(after)
    width = w_out.shape[1] // len(outs)
    copies = []
    for k in range(len(outs)):
        at = pl.ds(pl.multiple_of(lax.rem(place[2] + k, len(outs)) * width, width), width)
        copies.append(pltpu.make_async_copy(w_out.at[:, at], weights.at[k], sem.at[k]))
        copies[-1].start()
    for r, part in enumerate((a0, a1, a2, a3)):
        rows[lax.rem(place[0] + count - r, count)] = part[...]
    left = rows[...].reshape(count * span, depth)
    for k, out in enumerate(outs):
        copies[k].wait()
        for side in range(2):
            at = slice(side * width // 2, (side + 1) * width // 2)
            out[side] = jnp.dot(left, weights[k, :, at], preferred_element_type=F32).astype(
                out.dtype
            )


def project_out(place, parts, w_out, before):
    span, depth = parts[0].shape
    count = len(parts)
    width = w_out.shape[1] // 4
    vmem = pl.BlockSpec(memory_space=pltpu.VMEM)
    smem = pl.BlockSpec(memory_space=pltpu.SMEM)
    shape = (2, count * span, width // 2)
    return pl.pallas_call(
        output_kernel,
        in_specs=[smem] + [vmem] * count + [pl.BlockSpec(memory_space=pl.ANY)] * 2,
        out_specs=[vmem] * 5,
        out_shape=[jax.ShapeDtypeStruct(shape, F32)]
        + [jax.ShapeDtypeStruct(shape, BF)] * 3
        + [jax.ShapeDtypeStruct((8, 128), F32)],
        scratch_shapes=[
            pltpu.VMEM((count, span, depth), BF),
            pltpu.VMEM((4, depth, width), BF),
            pltpu.SemaphoreType.DMA((4,)),
        ],
        compiler_params=pltpu.CompilerParams(vmem_limit_bytes=24 * MIB),
        cost_estimate=pl.CostEstimate(
            flops=8 * count * span * depth * width, bytes_accessed=6 * MIB, transcendentals=0
        ),
        name="project_out",
    )(place, *parts, w_out, before)


def reduce_kernel(place, before, *refs):
    pieces, (send, keep) = refs[:-2], refs[-2:]
    for side, out in ((1 - place[3], send), (place[3], keep)):
        total = pieces[0][side].astype(F32)
        for piece in pieces[1:]:
            total = total + piece[side].astype(F32)
        out[...] = total.astype(out.dtype)


def reduce_pieces(place, before, pieces):
    _, rows, width = pieces[0].shape
    vmem = pl.BlockSpec(memory_space=pltpu.VMEM)
    return pl.pallas_call(
        reduce_kernel,
        in_specs=[pl.BlockSpec(memory_space=pltpu.SMEM), pl.BlockSpec(memory_space=pl.ANY)]
        + [vmem] * len(pieces),
        out_specs=[vmem] * 2,
        out_shape=[jax.ShapeDtypeStruct((rows, width), t) for t in (BF, F32)],
        compiler_params=pltpu.CompilerParams(vmem_limit_bytes=16 * MIB),
        cost_estimate=pl.CostEstimate(flops=8 * rows * width, bytes_accessed=16 * rows * width, transcendentals=0),
        name="reduce_pieces",
    )(place, before, *pieces)


def rotation(answer):
    half = HD // 2
    positions = (NBLK * BLOCK + jnp.arange(answer)).astype(F32)
    frequency = rope_base ** (-2.0 * jnp.arange(half).astype(F32) / HD)
    angles = positions[:, None] * frequency[None, :]
    cosine, sine = jnp.cos(angles), jnp.sin(angles)
    return jnp.concatenate([cosine, cosine], axis=1), jnp.concatenate([-sine, sine], axis=1)


def per_device(
    hidden, norm_gain, w_query, w_key, w_value, w_out, cache_key, cache_value, block_mask
):
    section = lax.axis_index("section")
    core = lax.rem(lax.axis_index("coal"), 2)
    tensor = lax.axis_index("tensor")
    z_hi = lax.rem(tensor, 2)
    quarter = lax.rem(lax.axis_index("coal"), 4)
    place = jnp.stack([section, core, tensor // 2, z_hi, quarter]).astype(jnp.int32)
    answer = hidden.shape[1]
    quarter_rows = cache_key.shape[0] // 4
    piece = jnp.stack(
        [
            lax.dynamic_slice_in_dim(cache_key, quarter * quarter_rows, quarter_rows, 0),
            lax.dynamic_slice_in_dim(cache_value, quarter * quarter_rows, quarter_rows, 0),
        ]
    )
    with jax.named_scope("cache"):
        mine = {r: section_shift(piece, r) for r in (1, 3)}
    with jax.named_scope("swap"):
        beside = {r: core_swap(mine[r]) for r in (1, 3)}
    with jax.named_scope("zcache"):
        over = {r: z_neighbour_swap(mine[r]) for r in (1, 3)}
    with jax.named_scope("zswap"):
        both = {r: core_swap(over[r]) for r in (1, 3)}
    with jax.named_scope("forward"):
        mine[2], over[2] = section_shift(mine[1], 1), section_shift(over[3], 3)
    with jax.named_scope("fswap"):
        beside[2], both[2] = core_swap(mine[2]), core_swap(over[2])
    pieces = [p[r] for r in (1, 2, 3) for p in (mine, beside, over, both)]
    cosine, sine = rotation(answer)

    chunks = project(place, hidden, norm_gain[None, :], w_query, w_key, w_value)
    with jax.named_scope("sums"):
        parts = [chunks[0]] + [section_shift(chunks[r], r) for r in (1, 3, 2)]
    queries, near_key, near_value = rotate(parts, cosine, sine)
    attended, gathered = [], []
    for h in range(HALVES):
        attention = attend(
            h, place, block_mask, queries, near_key, near_value, cache_key, cache_value, pieces
        )
        attended.append(attention)
        with jax.named_scope(f"gather{h}"):
            gathered.append([attention] + [section_shift(attention, r) for r in (1, 2, 3)])

    turn, send, results = attended[-1], queries, []
    for h in range(HALVES):
        *sums, turn = project_out(place, gathered[h], w_out, turn)
        with jax.named_scope(f"x{h}"):
            shares = [sums[0]] + [x_shift(sums[r], r) for r in (1, 2, 3)]
        send, keep = reduce_pieces(place, send, shares)
        with jax.named_scope(f"z{h}"):
            arrived = z_swap(send)
        result = (keep + arrived.astype(F32)).astype(BF)
        results.append(result.reshape(hidden.shape[0], answer // HALVES, -1))
    return jnp.concatenate(results, axis=1)


def solution(mesh):
    return jax.shard_map(
        per_device,
        mesh=mesh,
        in_specs=(
            P("coal", None, "section"),
            P("section"),
            P("section", "tensor"),
            P("section", "tensor"),
            P("section", "tensor"),
            P("tensor", "section"),
            P("section", "tensor"),
            P("section", "tensor"),
            P("coal", None),
        ),
        out_specs=P("coal", None, ("section", "tensor")),
        check_vma=False,
    )
```

```python
import functools
import math

import jax
import jax.numpy as jnp
from jax import lax
from jax.experimental import pallas as pl
from jax.experimental.pallas import tpu as pltpu
from jax.sharding import PartitionSpec as P

D = 8192
HD = 128
NBLK = 128
BLOCK = 64
rope_base = 500000.0
norm_eps = 1e-05
masked_score = -1e30
BF = jnp.bfloat16
F32 = jnp.float32
HALVES = 2
TILE = 1024
MIB = 1024 * 1024


def section_shift(x, by):
    n = lax.axis_size("section")
    return lax.ppermute(x, "section", [(i, (i + by) % n) for i in range(n)])


def x_shift(x, by):
    n = lax.axis_size("tensor") // 2
    return lax.ppermute(
        x, "tensor", [(i, ((i // 2 + by) % n) * 2 + i % 2) for i in range(2 * n)]
    )


def z_swap(x):
    return lax.ppermute(x, "tensor", [(i, i ^ 1) for i in range(lax.axis_size("tensor"))])


def core_swap(x):
    return lax.ppermute(x, "coal", [(i, i ^ 1) for i in range(lax.axis_size("coal"))])


def project_kernel(place, hidden, gain, w_query, w_key, w_value, *rest):
    outs, (rows, weights, scaled, product, sem) = rest[:-5], rest[-5:]
    count, answer, width = hidden.shape
    queries = w_query.shape[1]
    span = answer // HALVES
    steps, _, _, depth = rows.shape
    copies = []
    for k in range(steps):
        at = pl.ds(k * depth, depth)
        group = [
            (hidden.at[lax.rem(place[0] + r, count), :, at], rows.at[k, r]) for r in range(count)
        ]
        group += [
            (w_query.at[at], weights.at[at, pl.ds(0, queries)]),
            (w_key.at[at], weights.at[at, pl.ds(queries, HD)]),
            (w_value.at[at], weights.at[at, pl.ds(queries + HD, HD)]),
        ]
        copies.append(
            [pltpu.make_async_copy(a, b, sem.at[k, i]) for i, (a, b) in enumerate(group)]
        )
        for copy in copies[-1]:
            copy.start()

    squares = [jnp.zeros((answer, 128), F32) for _ in range(count)]
    for k in range(steps):
        at = slice(k * depth, (k + 1) * depth)
        for copy in copies[k]:
            copy.wait()
        for r in range(count):
            x = rows[k, r].astype(F32)
            x2 = x * x
            for j in range(depth // 128):
                squares[r] = squares[r] + x2[:, j * 128 : (j + 1) * 128]
            scaled[k, r * answer : (r + 1) * answer] = (x * gain[:, at]).astype(BF)
        partial = jnp.dot(scaled[k], weights[at], preferred_element_type=F32)
        if k == 0:
            product[...] = partial
        elif k < steps - 1:
            product[...] += partial
        else:
            partial = product[...] + partial
            lane = lax.broadcasted_iota(jnp.int32, (answer, 128), 1)
            for r in range(count):
                total = jnp.sum(squares[r], axis=-1, keepdims=True)
                high = total.astype(BF).astype(F32)
                pair = jnp.where(lane == 0, high, jnp.where(lane == 1, total - high, 0.0))
                for h in range(HALVES):
                    out = outs[r * HALVES + h]
                    start = r * answer + h * span
                    out[:, : queries + 2 * HD] = partial[start : start + span].astype(BF)
                    out[:, queries + 2 * HD :] = pair[h * span : (h + 1) * span].astype(BF)


def project(place, hidden, gain, w_query, w_key, w_value):
    count, answer, width = hidden.shape
    total = w_query.shape[1] + 2 * HD
    steps = 4
    smem = pl.BlockSpec(memory_space=pltpu.SMEM)
    vmem = pl.BlockSpec(memory_space=pltpu.VMEM)
    anywhere = pl.BlockSpec(memory_space=pl.ANY)
    return pl.pallas_call(
        project_kernel,
        in_specs=[smem, anywhere, vmem, anywhere, anywhere, anywhere],
        out_specs=[vmem] * (count * HALVES),
        out_shape=[jax.ShapeDtypeStruct((answer // HALVES, total + HD), BF)] * (count * HALVES),
        scratch_shapes=[
            pltpu.VMEM((steps, count, answer, width // steps), BF),
            pltpu.VMEM((width, total), BF),
            pltpu.VMEM((steps, count * answer, width // steps), BF),
            pltpu.VMEM((count * answer, total), F32),
            pltpu.SemaphoreType.DMA((steps, count + 3)),
        ],
        compiler_params=pltpu.CompilerParams(vmem_limit_bytes=60 * MIB),
        cost_estimate=pl.CostEstimate(
            flops=2 * count * answer * width * total, bytes_accessed=9 * MIB, transcendentals=0
        ),
        name="project",
    )(place, hidden, gain, w_query, w_key, w_value)


def attention_kernel(half, place, mask, p0, p1, p2, p3, cosine, sine, *rest):
    before, rest = (rest[:2], rest[2:]) if half else ((), rest)
    own_key, own_value, a1, b1, a3, b3, key2, value2, key2b, value2b, out, *rest = rest
    after, rest = ([], rest) if half == HALVES - 1 else (rest[:2], rest[2:])
    queries, near_key, near_value, keys, values, buf0, buf1, sem = rest
    section, core = place[0], place[1]
    span = p0.shape[0]
    answer = near_key.shape[0]
    heads = out.shape[1] // HD
    rows = heads * span
    local = own_key.shape[0]
    piece_rows = local // 2
    sections = keys.shape[0] // local

    copies = []

    def bring(source, buffer, start, size):
        copy = pltpu.make_async_copy(
            source,
            buffer.at[pl.ds(pl.multiple_of(start, size), size), pl.ds(0, HD)],
            sem.at[len(copies)],
        )
        copy.start()
        copies.append(copy)

    bring(own_key, keys, section * local, local)
    bring(own_value, values, section * local, local)
    pairs = [(r, p.at[0], p.at[1]) for r, p in ((1, a1), (1, b1), (3, a3), (3, b3))]
    pairs += [(2, key2, value2), (2, key2b, value2b)]
    for n, (r, *pair) in enumerate(pairs):
        source = lax.rem(section + sections - r, sections)
        side = core if n % 2 == 0 else 1 - core
        for piece, buffer in zip(pair, (keys, values)):
            bring(piece, buffer, source * local + side * piece_rows, piece_rows)

    first = jnp.where(lax.broadcasted_iota(jnp.int32, (rows, HD), 1) == 0, 1.0, 0.0).astype(BF)

    def fill(b, carry):
        at = pl.ds(pl.multiple_of(b * BLOCK, BLOCK), BLOCK)
        bias = jnp.where(mask[section, b] > 0, 0.0, masked_score)
        keys[at, HD:] = jnp.full((BLOCK, HD), bias, F32).astype(BF)
        values[at, HD:] = first[:BLOCK]
        return carry

    lax.fori_loop(0, keys.shape[0] // BLOCK, fill, 0, unroll=4)

    width = (heads + 2) * HD
    total = (
        p0[:, width:].astype(F32) + p1[:, width:].astype(F32)
        + p2[:, width:].astype(F32) + p3[:, width:].astype(F32)
    )
    scale = lax.rsqrt((total[:, 0:1] + total[:, 1:2]) / D + norm_eps)

    def column(h):
        at = slice(h * HD, (h + 1) * HD)
        return (
            p0[:, at].astype(F32) + p1[:, at].astype(F32)
            + p2[:, at].astype(F32) + p3[:, at].astype(F32)
        ) * scale

    def turned(x):
        return x * cosine[...] + pltpu.roll(x, HD // 2, 1) * sine[...]

    factor = math.log2(math.e) / math.sqrt(HD)
    for h in range(heads):
        queries[h * span : (h + 1) * span] = (turned(column(h)) * factor).astype(BF)
    new_key = turned(column(heads)).astype(BF)
    new_value = column(heads + 1).astype(BF)
    for ref, new in zip(after, (new_key, new_value)):
        ref[...] = new
    near_value[:, HD:] = first[:answer]
    for h in range(HALVES):
        at = slice(h * span, (h + 1) * span)
        if h == half:
            near_key[at], near_value[at, :HD] = new_key, new_value
        elif h < half:
            near_key[at], near_value[at, :HD] = before[0][...], before[1][...]
        else:
            near_key[at] = jnp.zeros((span, HD), BF)
            near_value[at, :HD] = jnp.zeros((span, HD), BF)

    tile = buf0.shape[1]
    tiles = keys.shape[0] // tile
    dims = (((1,), (1,)), ((), ()))
    q = queries[...]
    q_aug = jnp.concatenate([q, first], axis=1)
    s = lax.dot_general(q, near_key[...], dims, preferred_element_type=F32)
    row = lax.rem(lax.broadcasted_iota(jnp.int32, (rows, answer), 0), span) + half * span
    s = jnp.where(row >= lax.broadcasted_iota(jnp.int32, (rows, answer), 1), s, masked_score)
    m = jnp.max(s, axis=-1, keepdims=True)
    acc = jnp.dot(jnp.exp2(s - m).astype(BF), near_value[...], preferred_element_type=F32)

    for copy in copies:
        copy.wait()

    def score(t, buffer):
        at = pl.ds(pl.multiple_of(t * tile, tile), tile)
        s = lax.dot_general(q_aug, keys[at], dims, preferred_element_type=F32)
        buffer[...] = s
        return jnp.max(s, axis=-1, keepdims=True)

    def weigh(t, buffer, m, m_new, acc):
        at = pl.ds(pl.multiple_of(t * tile, tile), tile)
        p = jnp.exp2(buffer[...] - m_new).astype(BF)
        return acc * jnp.exp2(m - m_new) + jnp.dot(p, values[at], preferred_element_type=F32)

    def pair(i, state):
        m, top, acc = state
        t = 2 * i
        m_new = jnp.maximum(m, top)
        top = score(t + 1, buf1)
        acc = weigh(t, buf0, m, m_new, acc)
        m = m_new
        m_new = jnp.maximum(m, top)
        top = score(lax.rem(t + 2, tiles), buf0)
        acc = weigh(t + 1, buf1, m, m_new, acc)
        return m_new, top, acc

    m, _, acc = lax.fori_loop(0, tiles // 2, pair, (m, score(0, buf0), acc))
    result = (acc[:, :HD] / acc[:, HD : HD + 1]).astype(BF)
    for h in range(heads):
        out[:, h * HD : (h + 1) * HD] = result[h * span : (h + 1) * span]


def attend(half, place, mask, parts, cosine, sine, before, own_key, own_value, pieces):
    span = parts[0].shape[0]
    answer = span * HALVES
    context = NBLK * BLOCK
    heads = parts[0].shape[1] // HD - 3
    rows = heads * span
    vmem = pl.BlockSpec(memory_space=pltpu.VMEM)
    smem = pl.BlockSpec(memory_space=pltpu.SMEM)
    anywhere = pl.BlockSpec(memory_space=pl.ANY)
    extra = 0 if half == HALVES - 1 else 2
    outs = [jax.ShapeDtypeStruct((span, heads * HD), BF)]
    outs += [jax.ShapeDtypeStruct((span, HD), BF)] * extra
    return pl.pallas_call(
        functools.partial(attention_kernel, half),
        in_specs=[smem, smem] + [vmem] * (6 + len(before)) + [anywhere] * 10,
        out_specs=[vmem] * (1 + extra),
        out_shape=outs,
        scratch_shapes=[
            pltpu.VMEM((rows, HD), BF),
            pltpu.VMEM((answer, HD), BF),
            pltpu.VMEM((answer, 2 * HD), BF),
            pltpu.VMEM((context, 2 * HD), BF),
            pltpu.VMEM((context, 2 * HD), BF),
            pltpu.VMEM((rows, TILE), F32),
            pltpu.VMEM((rows, TILE), F32),
            pltpu.SemaphoreType.DMA((14,)),
        ],
        compiler_params=pltpu.CompilerParams(vmem_limit_bytes=32 * MIB),
        cost_estimate=pl.CostEstimate(
            flops=8 * rows * context * HD,
            bytes_accessed=6 * MIB,
            transcendentals=rows * context,
        ),
        name="attend",
    )(place, mask, *parts, cosine, sine, *before, own_key, own_value, *pieces)


def output_kernel(place, a0, a1, a2, a3, w_out, before, o0, o1, o2, o3, after, rows, weights, sem):
    count, span, depth = rows.shape
    outs = (o0, o1, o2, o3)
    after[...] = jnp.zeros_like(after)
    width = w_out.shape[1] // len(outs)
    copies = []
    for k in range(len(outs)):
        at = pl.ds(pl.multiple_of(lax.rem(place[2] + k, len(outs)) * width, width), width)
        copies.append(pltpu.make_async_copy(w_out.at[:, at], weights.at[k], sem.at[k]))
        copies[-1].start()
    for r, part in enumerate((a0, a1, a2, a3)):
        rows[lax.rem(place[0] + count - r, count)] = part[...]
    left = rows[...].reshape(count * span, depth)
    for k, out in enumerate(outs):
        copies[k].wait()
        for side in range(2):
            at = slice(side * width // 2, (side + 1) * width // 2)
            out[side] = jnp.dot(left, weights[k, :, at], preferred_element_type=F32).astype(
                out.dtype
            )


def project_out(place, parts, w_out, before):
    span, depth = parts[0].shape
    count = len(parts)
    width = w_out.shape[1] // 4
    vmem = pl.BlockSpec(memory_space=pltpu.VMEM)
    smem = pl.BlockSpec(memory_space=pltpu.SMEM)
    shape = (2, count * span, width // 2)
    return pl.pallas_call(
        output_kernel,
        in_specs=[smem] + [vmem] * count + [pl.BlockSpec(memory_space=pl.ANY)] * 2,
        out_specs=[vmem] * 5,
        out_shape=[jax.ShapeDtypeStruct(shape, F32)]
        + [jax.ShapeDtypeStruct(shape, BF)] * 3
        + [jax.ShapeDtypeStruct((8, 128), F32)],
        scratch_shapes=[
            pltpu.VMEM((count, span, depth), BF),
            pltpu.VMEM((4, depth, width), BF),
            pltpu.SemaphoreType.DMA((4,)),
        ],
        compiler_params=pltpu.CompilerParams(vmem_limit_bytes=24 * MIB),
        cost_estimate=pl.CostEstimate(
            flops=8 * count * span * depth * width, bytes_accessed=6 * MIB, transcendentals=0
        ),
        name="project_out",
    )(place, *parts, w_out, before)


def reduce_kernel(place, before, *refs):
    pieces, (send, keep) = refs[:-2], refs[-2:]
    for side, out in ((1 - place[3], send), (place[3], keep)):
        total = pieces[0][side].astype(F32)
        for piece in pieces[1:]:
            total = total + piece[side].astype(F32)
        out[...] = total.astype(out.dtype)


def reduce_pieces(place, before, pieces):
    _, rows, width = pieces[0].shape
    vmem = pl.BlockSpec(memory_space=pltpu.VMEM)
    return pl.pallas_call(
        reduce_kernel,
        in_specs=[pl.BlockSpec(memory_space=pltpu.SMEM), pl.BlockSpec(memory_space=pl.ANY)]
        + [vmem] * len(pieces),
        out_specs=[vmem] * 2,
        out_shape=[jax.ShapeDtypeStruct((rows, width), t) for t in (BF, F32)],
        compiler_params=pltpu.CompilerParams(vmem_limit_bytes=16 * MIB),
        cost_estimate=pl.CostEstimate(flops=8 * rows * width, bytes_accessed=16 * rows * width, transcendentals=0),
        name="reduce_pieces",
    )(place, before, *pieces)


def finish_kernel(earlier, keep, arrived, out):
    count, rows, _ = out.shape
    start = earlier.shape[1]
    out[:, :start] = earlier[...]
    total = (keep[...] + arrived[...].astype(F32)).astype(out.dtype)
    for c in range(count):
        out[c, start:] = total[c * (rows - start) : (c + 1) * (rows - start)]


def finish(earlier, keep, arrived):
    count, rows, width = earlier.shape
    vmem = pl.BlockSpec(memory_space=pltpu.VMEM)
    return pl.pallas_call(
        finish_kernel,
        in_specs=[vmem] * 3,
        out_specs=vmem,
        out_shape=jax.ShapeDtypeStruct((count, rows + keep.shape[0] // count, width), BF),
        compiler_params=pltpu.CompilerParams(vmem_limit_bytes=16 * MIB),
        name="finish",
    )(earlier, keep, arrived)


def rotation(answer):
    half = HD // 2
    positions = (NBLK * BLOCK + jnp.arange(answer)).astype(F32)
    frequency = rope_base ** (-2.0 * jnp.arange(half).astype(F32) / HD)
    angles = positions[:, None] * frequency[None, :]
    cosine, sine = jnp.cos(angles), jnp.sin(angles)
    return jnp.concatenate([cosine, cosine], axis=1), jnp.concatenate([-sine, sine], axis=1)


def per_device(
    hidden, norm_gain, w_query, w_key, w_value, w_out, cache_key, cache_value, block_mask
):
    section = lax.axis_index("section")
    core = lax.rem(lax.axis_index("coal"), 2)
    tensor = lax.axis_index("tensor")
    z_hi = lax.rem(tensor, 2)
    place = jnp.stack([section, core, tensor // 2, z_hi]).astype(jnp.int32)
    answer = hidden.shape[1]
    span = answer // HALVES
    half_rows = cache_key.shape[0] // 2
    piece = jnp.stack(
        [
            lax.dynamic_slice_in_dim(cache_key, core * half_rows, half_rows, 0),
            lax.dynamic_slice_in_dim(cache_value, core * half_rows, half_rows, 0),
        ]
    )
    with jax.named_scope("cache"):
        mine1, mine3 = section_shift(piece, 1), section_shift(piece, 3)
    with jax.named_scope("forward"):
        key2, value2 = section_shift(mine1[0], 1), section_shift(mine3[1], 3)
    with jax.named_scope("swap"):
        pieces = (mine1, core_swap(mine1), mine3, core_swap(mine3))
        pieces += (key2, value2, core_swap(key2), core_swap(value2))
    cosine, sine = rotation(answer)

    chunks = project(place, hidden, norm_gain[None, :], w_query, w_key, w_value)
    parts = []
    for h in range(HALVES):
        with jax.named_scope(f"sums{h}"):
            parts.append(
                [chunks[h]] + [section_shift(chunks[r * HALVES + h], r) for r in (1, 2, 3)]
            )
    before, attended, gathered = [], [], []
    for h in range(HALVES):
        at = slice(h * span, (h + 1) * span)
        attention, *before = attend(
            h, place, block_mask, parts[h], cosine[at], sine[at], before,
            cache_key, cache_value, pieces,
        )
        attended.append(attention)
        with jax.named_scope(f"gather{h}"):
            gathered.append([attention] + [section_shift(attention, r) for r in (1, 2, 3)])

    turn, send = attended[-1], attended[0]
    for h in range(HALVES):
        *sums, turn = project_out(place, gathered[h], w_out, turn)
        with jax.named_scope(f"x{h}"):
            pieces = [sums[0]] + [x_shift(sums[r], r) for r in (1, 2, 3)]
        send, keep = reduce_pieces(place, send, pieces)
        with jax.named_scope(f"z{h}"):
            arrived = z_swap(send)
        if h == 0:
            result = (keep + arrived.astype(F32)).astype(BF)
            result = result.reshape(hidden.shape[0], answer // HALVES, -1)
        else:
            result = finish(result, keep, arrived)
    return result


def solution(mesh):
    return jax.shard_map(
        per_device,
        mesh=mesh,
        in_specs=(
            P("coal", None, "section"),
            P("section"),
            P("section", "tensor"),
            P("section", "tensor"),
            P("section", "tensor"),
            P("tensor", "section"),
            P("section", "tensor"),
            P("section", "tensor"),
            P("coal", None),
        ),
        out_specs=P("coal", None, ("section", "tensor")),
        check_vma=False,
    )
```

```python
import functools
import math

import jax
import jax.numpy as jnp
from jax import lax
from jax.experimental import pallas as pl
from jax.experimental.pallas import tpu as pltpu
from jax.sharding import PartitionSpec as P

D = 8192
HD = 128
NBLK = 128
BLOCK = 64
rope_base = 500000.0
norm_eps = 1e-05
masked_score = -1e30
BF = jnp.bfloat16
F32 = jnp.float32
HALVES = 2
TILE = 1024
LOOPS = 2
MIB = 1024 * 1024


def section_shift(x, by):
    n = lax.axis_size("section")
    return lax.ppermute(x, "section", [(i, (i + by) % n) for i in range(n)])


def x_shift(x, by):
    n = lax.axis_size("tensor") // 2
    return lax.ppermute(
        x, "tensor", [(i, ((i // 2 + by) % n) * 2 + i % 2) for i in range(2 * n)]
    )


def z_swap(x):
    return lax.ppermute(x, "tensor", [(i, i ^ 1) for i in range(lax.axis_size("tensor"))])


def core_swap(x):
    return lax.ppermute(x, "coal", [(i, i ^ 1) for i in range(lax.axis_size("coal"))])


def project_kernel(place, hidden, gain, w_query, w_key, w_value, *rest):
    outs, (rows, weights, scaled, product, sem) = rest[:-5], rest[-5:]
    count, answer, width = hidden.shape
    queries = w_query.shape[1]
    span = answer // HALVES
    steps, _, _, depth = rows.shape
    copies = []
    for k in range(steps):
        at = pl.ds(k * depth, depth)
        group = [
            (hidden.at[lax.rem(place[0] + r, count), :, at], rows.at[k, r]) for r in range(count)
        ]
        group += [
            (w_query.at[at], weights.at[at, pl.ds(0, queries)]),
            (w_key.at[at], weights.at[at, pl.ds(queries, HD)]),
            (w_value.at[at], weights.at[at, pl.ds(queries + HD, HD)]),
        ]
        copies.append(
            [pltpu.make_async_copy(a, b, sem.at[k, i]) for i, (a, b) in enumerate(group)]
        )
        for copy in copies[-1]:
            copy.start()

    squares = [jnp.zeros((answer, 128), F32) for _ in range(count)]
    for k in range(steps):
        at = slice(k * depth, (k + 1) * depth)
        for copy in copies[k]:
            copy.wait()
        for r in range(count):
            x = rows[k, r].astype(F32)
            x2 = x * x
            for j in range(depth // 128):
                squares[r] = squares[r] + x2[:, j * 128 : (j + 1) * 128]
            scaled[k, r * answer : (r + 1) * answer] = (x * gain[:, at]).astype(BF)
        partial = jnp.dot(scaled[k], weights[at], preferred_element_type=F32)
        if k == 0:
            product[...] = partial
        elif k < steps - 1:
            product[...] += partial
        else:
            partial = product[...] + partial
            lane = lax.broadcasted_iota(jnp.int32, (answer, 128), 1)
            for r in range(count):
                total = jnp.sum(squares[r], axis=-1, keepdims=True)
                high = total.astype(BF).astype(F32)
                pair = jnp.where(lane == 0, high, jnp.where(lane == 1, total - high, 0.0))
                for h in range(HALVES):
                    out = outs[r * HALVES + h]
                    start = r * answer + h * span
                    out[:, : queries + 2 * HD] = partial[start : start + span].astype(BF)
                    out[:, queries + 2 * HD :] = pair[h * span : (h + 1) * span].astype(BF)


def project(place, hidden, gain, w_query, w_key, w_value):
    count, answer, width = hidden.shape
    total = w_query.shape[1] + 2 * HD
    steps = 4
    smem = pl.BlockSpec(memory_space=pltpu.SMEM)
    vmem = pl.BlockSpec(memory_space=pltpu.VMEM)
    anywhere = pl.BlockSpec(memory_space=pl.ANY)
    return pl.pallas_call(
        project_kernel,
        in_specs=[smem, anywhere, vmem, anywhere, anywhere, anywhere],
        out_specs=[vmem] * (count * HALVES),
        out_shape=[jax.ShapeDtypeStruct((answer // HALVES, total + HD), BF)] * (count * HALVES),
        scratch_shapes=[
            pltpu.VMEM((steps, count, answer, width // steps), BF),
            pltpu.VMEM((width, total), BF),
            pltpu.VMEM((steps, count * answer, width // steps), BF),
            pltpu.VMEM((count * answer, total), F32),
            pltpu.SemaphoreType.DMA((steps, count + 3)),
        ],
        compiler_params=pltpu.CompilerParams(vmem_limit_bytes=60 * MIB),
        cost_estimate=pl.CostEstimate(
            flops=2 * count * answer * width * total, bytes_accessed=9 * MIB, transcendentals=0
        ),
        name="project",
    )(place, hidden, gain, w_query, w_key, w_value)


def attention_kernel(half, place, mask, p0, p1, p2, p3, cosine, sine, *rest):
    before, rest = (rest[:2], rest[2:]) if half else ((), rest)
    own_key, own_value, a1, b1, a3, b3, key2, value2, key2b, value2b, out, *rest = rest
    after, rest = ([], rest) if half == HALVES - 1 else (rest[:2], rest[2:])
    queries, near_key, near_value, keys, values, buf0, buf1, sem = rest
    section, core = place[0], place[1]
    span = p0.shape[0]
    answer = near_key.shape[0]
    heads = out.shape[1] // HD
    rows = heads * span
    local = own_key.shape[0]
    piece_rows = local // 2
    sections = keys.shape[0] // local

    copies = []

    def bring(source, buffer, start, size):
        copy = pltpu.make_async_copy(
            source,
            buffer.at[pl.ds(pl.multiple_of(start, size), size), pl.ds(0, HD)],
            sem.at[len(copies)],
        )
        copy.start()
        copies.append(copy)

    bring(own_key, keys, section * local, local)
    bring(own_value, values, section * local, local)
    pairs = [(r, p.at[0], p.at[1]) for r, p in ((1, a1), (1, b1), (3, a3), (3, b3))]
    pairs += [(2, key2, value2), (2, key2b, value2b)]
    for n, (r, *pair) in enumerate(pairs):
        source = lax.rem(section + sections - r, sections)
        side = core if n % 2 == 0 else 1 - core
        for piece, buffer in zip(pair, (keys, values)):
            bring(piece, buffer, source * local + side * piece_rows, piece_rows)

    first = jnp.where(lax.broadcasted_iota(jnp.int32, (rows, HD), 1) == 0, 1.0, 0.0).astype(BF)

    def fill(b, carry):
        at = pl.ds(pl.multiple_of(b * BLOCK, BLOCK), BLOCK)
        bias = jnp.where(mask[section, b] > 0, 0.0, masked_score)
        keys[at, HD:] = jnp.full((BLOCK, HD), bias, F32).astype(BF)
        values[at, HD:] = first[:BLOCK]
        return carry

    lax.fori_loop(0, keys.shape[0] // BLOCK, fill, 0, unroll=4)

    width = (heads + 2) * HD
    total = (
        p0[:, width:].astype(F32) + p1[:, width:].astype(F32)
        + p2[:, width:].astype(F32) + p3[:, width:].astype(F32)
    )
    scale = lax.rsqrt((total[:, 0:1] + total[:, 1:2]) / D + norm_eps)

    def column(h):
        at = slice(h * HD, (h + 1) * HD)
        return (
            p0[:, at].astype(F32) + p1[:, at].astype(F32)
            + p2[:, at].astype(F32) + p3[:, at].astype(F32)
        ) * scale

    def turned(x):
        return x * cosine[...] + pltpu.roll(x, HD // 2, 1) * sine[...]

    factor = math.log2(math.e) / math.sqrt(HD)
    for h in range(heads):
        queries[h * span : (h + 1) * span] = (turned(column(h)) * factor).astype(BF)
    new_key = turned(column(heads)).astype(BF)
    new_value = column(heads + 1).astype(BF)
    for ref, new in zip(after, (new_key, new_value)):
        ref[...] = new
    near_value[:, HD:] = first[:answer]
    for h in range(HALVES):
        at = slice(h * span, (h + 1) * span)
        if h == half:
            near_key[at], near_value[at, :HD] = new_key, new_value
        elif h < half:
            near_key[at], near_value[at, :HD] = before[0][...], before[1][...]
        else:
            near_key[at] = jnp.zeros((span, HD), BF)
            near_value[at, :HD] = jnp.zeros((span, HD), BF)

    tile = buf0.shape[1]
    tiles = keys.shape[0] // tile
    dims = (((1,), (1,)), ((), ()))
    q = queries[...]
    q_aug = jnp.concatenate([q, first], axis=1)
    s = lax.dot_general(q, near_key[...], dims, preferred_element_type=F32)
    row = lax.rem(lax.broadcasted_iota(jnp.int32, (rows, answer), 0), span) + half * span
    s = jnp.where(row >= lax.broadcasted_iota(jnp.int32, (rows, answer), 1), s, masked_score)
    m = jnp.max(s, axis=-1, keepdims=True)
    acc = jnp.dot(jnp.exp2(s - m).astype(BF), near_value[...], preferred_element_type=F32)

    for copy in copies:
        copy.wait()

    buffers = (buf0, buf1)
    each = tiles // LOOPS

    def at(t):
        return pl.ds(pl.multiple_of(t * tile, tile), tile)

    def sweep(i, state):
        m, acc = state

        def score(t):
            s = lax.dot_general(
                q_aug, keys[at(i * each + t)], dims, preferred_element_type=F32
            )
            buffers[t % 2][...] = s
            return jnp.max(s, axis=-1, keepdims=True)

        top = score(0)
        for t in range(each):
            m_new = jnp.maximum(m, top)
            if t + 1 < each:
                top = score(t + 1)
            p = jnp.exp2(buffers[t % 2][...] - m_new).astype(BF)
            acc = acc * jnp.exp2(m - m_new) + jnp.dot(
                p, values[at(i * each + t)], preferred_element_type=F32
            )
            m = m_new
        return m, acc

    m, acc = lax.fori_loop(0, LOOPS, sweep, (m, acc))
    result = (acc[:, :HD] / acc[:, HD : HD + 1]).astype(BF)
    for h in range(heads):
        out[:, h * HD : (h + 1) * HD] = result[h * span : (h + 1) * span]


def attend(half, place, mask, parts, cosine, sine, before, own_key, own_value, pieces):
    span = parts[0].shape[0]
    answer = span * HALVES
    context = NBLK * BLOCK
    heads = parts[0].shape[1] // HD - 3
    rows = heads * span
    vmem = pl.BlockSpec(memory_space=pltpu.VMEM)
    smem = pl.BlockSpec(memory_space=pltpu.SMEM)
    anywhere = pl.BlockSpec(memory_space=pl.ANY)
    extra = 0 if half == HALVES - 1 else 2
    outs = [jax.ShapeDtypeStruct((span, heads * HD), BF)]
    outs += [jax.ShapeDtypeStruct((span, HD), BF)] * extra
    return pl.pallas_call(
        functools.partial(attention_kernel, half),
        in_specs=[smem, smem] + [vmem] * (6 + len(before)) + [anywhere] * 10,
        out_specs=[vmem] * (1 + extra),
        out_shape=outs,
        scratch_shapes=[
            pltpu.VMEM((rows, HD), BF),
            pltpu.VMEM((answer, HD), BF),
            pltpu.VMEM((answer, 2 * HD), BF),
            pltpu.VMEM((context, 2 * HD), BF),
            pltpu.VMEM((context, 2 * HD), BF),
            pltpu.VMEM((rows, TILE), F32),
            pltpu.VMEM((rows, TILE), F32),
            pltpu.SemaphoreType.DMA((14,)),
        ],
        compiler_params=pltpu.CompilerParams(vmem_limit_bytes=32 * MIB),
        cost_estimate=pl.CostEstimate(
            flops=8 * rows * context * HD,
            bytes_accessed=6 * MIB,
            transcendentals=rows * context,
        ),
        name="attend",
    )(place, mask, *parts, cosine, sine, *before, own_key, own_value, *pieces)


def output_kernel(place, a0, a1, a2, a3, w_out, before, o0, o1, o2, o3, after, rows, weights, sem):
    count, span, depth = rows.shape
    outs = (o0, o1, o2, o3)
    after[...] = jnp.zeros_like(after)
    width = w_out.shape[1] // len(outs)
    copies = []
    for k in range(len(outs)):
        at = pl.ds(pl.multiple_of(lax.rem(place[2] + k, len(outs)) * width, width), width)
        copies.append(pltpu.make_async_copy(w_out.at[:, at], weights.at[k], sem.at[k]))
        copies[-1].start()
    for r, part in enumerate((a0, a1, a2, a3)):
        rows[lax.rem(place[0] + count - r, count)] = part[...]
    left = rows[...].reshape(count * span, depth)
    for k, out in enumerate(outs):
        copies[k].wait()
        for side in range(2):
            at = slice(side * width // 2, (side + 1) * width // 2)
            out[side] = jnp.dot(left, weights[k, :, at], preferred_element_type=F32).astype(
                out.dtype
            )


def project_out(place, parts, w_out, before):
    span, depth = parts[0].shape
    count = len(parts)
    width = w_out.shape[1] // 4
    vmem = pl.BlockSpec(memory_space=pltpu.VMEM)
    smem = pl.BlockSpec(memory_space=pltpu.SMEM)
    shape = (2, count * span, width // 2)
    return pl.pallas_call(
        output_kernel,
        in_specs=[smem] + [vmem] * count + [pl.BlockSpec(memory_space=pl.ANY)] * 2,
        out_specs=[vmem] * 5,
        out_shape=[jax.ShapeDtypeStruct(shape, F32)]
        + [jax.ShapeDtypeStruct(shape, BF)] * 3
        + [jax.ShapeDtypeStruct((8, 128), F32)],
        scratch_shapes=[
            pltpu.VMEM((count, span, depth), BF),
            pltpu.VMEM((4, depth, width), BF),
            pltpu.SemaphoreType.DMA((4,)),
        ],
        compiler_params=pltpu.CompilerParams(vmem_limit_bytes=24 * MIB),
        cost_estimate=pl.CostEstimate(
            flops=8 * count * span * depth * width, bytes_accessed=6 * MIB, transcendentals=0
        ),
        name="project_out",
    )(place, *parts, w_out, before)


def reduce_kernel(place, before, *refs):
    pieces, (send, keep) = refs[:-2], refs[-2:]
    for side, out in ((1 - place[3], send), (place[3], keep)):
        total = pieces[0][side].astype(F32)
        for piece in pieces[1:]:
            total = total + piece[side].astype(F32)
        out[...] = total.astype(out.dtype)


def reduce_pieces(place, before, pieces):
    _, rows, width = pieces[0].shape
    vmem = pl.BlockSpec(memory_space=pltpu.VMEM)
    return pl.pallas_call(
        reduce_kernel,
        in_specs=[pl.BlockSpec(memory_space=pltpu.SMEM), pl.BlockSpec(memory_space=pl.ANY)]
        + [vmem] * len(pieces),
        out_specs=[vmem] * 2,
        out_shape=[jax.ShapeDtypeStruct((rows, width), t) for t in (BF, F32)],
        compiler_params=pltpu.CompilerParams(vmem_limit_bytes=16 * MIB),
        cost_estimate=pl.CostEstimate(flops=8 * rows * width, bytes_accessed=16 * rows * width, transcendentals=0),
        name="reduce_pieces",
    )(place, before, *pieces)


def finish_kernel(earlier, keep, arrived, out):
    count, rows, _ = out.shape
    start = earlier.shape[1]
    out[:, :start] = earlier[...]
    total = (keep[...] + arrived[...].astype(F32)).astype(out.dtype)
    for c in range(count):
        out[c, start:] = total[c * (rows - start) : (c + 1) * (rows - start)]


def finish(earlier, keep, arrived):
    count, rows, width = earlier.shape
    vmem = pl.BlockSpec(memory_space=pltpu.VMEM)
    return pl.pallas_call(
        finish_kernel,
        in_specs=[vmem] * 3,
        out_specs=vmem,
        out_shape=jax.ShapeDtypeStruct((count, rows + keep.shape[0] // count, width), BF),
        compiler_params=pltpu.CompilerParams(vmem_limit_bytes=16 * MIB),
        name="finish",
    )(earlier, keep, arrived)


def rotation(answer):
    half = HD // 2
    positions = (NBLK * BLOCK + jnp.arange(answer)).astype(F32)
    frequency = rope_base ** (-2.0 * jnp.arange(half).astype(F32) / HD)
    angles = positions[:, None] * frequency[None, :]
    cosine, sine = jnp.cos(angles), jnp.sin(angles)
    return jnp.concatenate([cosine, cosine], axis=1), jnp.concatenate([-sine, sine], axis=1)


def per_device(
    hidden, norm_gain, w_query, w_key, w_value, w_out, cache_key, cache_value, block_mask
):
    section = lax.axis_index("section")
    core = lax.rem(lax.axis_index("coal"), 2)
    tensor = lax.axis_index("tensor")
    z_hi = lax.rem(tensor, 2)
    place = jnp.stack([section, core, tensor // 2, z_hi]).astype(jnp.int32)
    answer = hidden.shape[1]
    span = answer // HALVES
    half_rows = cache_key.shape[0] // 2
    piece = jnp.stack(
        [
            lax.dynamic_slice_in_dim(cache_key, core * half_rows, half_rows, 0),
            lax.dynamic_slice_in_dim(cache_value, core * half_rows, half_rows, 0),
        ]
    )
    with jax.named_scope("cache"):
        mine1, mine3 = section_shift(piece, 1), section_shift(piece, 3)
    with jax.named_scope("forward"):
        key2, value2 = section_shift(mine1[0], 1), section_shift(mine3[1], 3)
    with jax.named_scope("swap"):
        pieces = (mine1, core_swap(mine1), mine3, core_swap(mine3))
        pieces += (key2, value2, core_swap(key2), core_swap(value2))
    cosine, sine = rotation(answer)

    chunks = project(place, hidden, norm_gain[None, :], w_query, w_key, w_value)
    parts = []
    for h in range(HALVES):
        with jax.named_scope(f"sums{h}"):
            parts.append(
                [chunks[h]] + [section_shift(chunks[r * HALVES + h], r) for r in (2, 1, 3)]
            )
    before, attended, gathered = [], [], []
    for h in range(HALVES):
        at = slice(h * span, (h + 1) * span)
        attention, *before = attend(
            h, place, block_mask, parts[h], cosine[at], sine[at], before,
            cache_key, cache_value, pieces,
        )
        attended.append(attention)
        with jax.named_scope(f"gather{h}"):
            gathered.append([attention] + [section_shift(attention, r) for r in (1, 2, 3)])

    turn, send = attended[-1], attended[0]
    for h in range(HALVES):
        *sums, turn = project_out(place, gathered[h], w_out, turn)
        with jax.named_scope(f"x{h}"):
            pieces = [sums[0]] + [x_shift(sums[r], r) for r in (2, 1, 3)]
        send, keep = reduce_pieces(place, send, pieces)
        with jax.named_scope(f"z{h}"):
            arrived = z_swap(send)
        if h == 0:
            result = (keep + arrived.astype(F32)).astype(BF)
            result = result.reshape(hidden.shape[0], answer // HALVES, -1)
        else:
            result = finish(result, keep, arrived)
    return result


def solution(mesh):
    return jax.shard_map(
        per_device,
        mesh=mesh,
        in_specs=(
            P("coal", None, "section"),
            P("section"),
            P("section", "tensor"),
            P("section", "tensor"),
            P("section", "tensor"),
            P("tensor", "section"),
            P("section", "tensor"),
            P("section", "tensor"),
            P("coal", None),
        ),
        out_specs=P("coal", None, ("section", "tensor")),
        check_vma=False,
    )
```

```python
import functools
import math

import jax
import jax.numpy as jnp
from jax import lax
from jax.experimental import pallas as pl
from jax.experimental.pallas import tpu as pltpu
from jax.sharding import PartitionSpec as P

D = 8192
HD = 128
NBLK = 128
BLOCK = 64
rope_base = 500000.0
norm_eps = 1e-05
masked_score = -1e30
BF = jnp.bfloat16
F32 = jnp.float32
HALVES = 2
TILE = 1024
LOOPS = 2
MIB = 1024 * 1024


def section_shift(x, by):
    n = lax.axis_size("section")
    return lax.ppermute(x, "section", [(i, (i + by) % n) for i in range(n)])


def x_shift(x, by):
    n = lax.axis_size("tensor") // 2
    return lax.ppermute(
        x, "tensor", [(i, ((i // 2 + by) % n) * 2 + i % 2) for i in range(2 * n)]
    )


def z_swap(x):
    return lax.ppermute(x, "tensor", [(i, i ^ 1) for i in range(lax.axis_size("tensor"))])


def core_swap(x):
    return lax.ppermute(x, "coal", [(i, i ^ 1) for i in range(lax.axis_size("coal"))])


def project_kernel(place, hidden, gain, w_query, w_key, w_value, *rest):
    outs, (rows, weights, scaled, product, sem) = rest[:-5], rest[-5:]
    count, answer, width = hidden.shape
    queries = w_query.shape[1]
    span = answer // HALVES
    steps, _, _, depth = rows.shape
    copies = []
    for k in range(steps):
        at = pl.ds(k * depth, depth)
        group = [
            (hidden.at[lax.rem(place[0] + r, count), :, at], rows.at[k, r]) for r in range(count)
        ]
        group += [
            (w_query.at[at], weights.at[at, pl.ds(0, queries)]),
            (w_key.at[at], weights.at[at, pl.ds(queries, HD)]),
            (w_value.at[at], weights.at[at, pl.ds(queries + HD, HD)]),
        ]
        copies.append(
            [pltpu.make_async_copy(a, b, sem.at[k, i]) for i, (a, b) in enumerate(group)]
        )
        for copy in copies[-1]:
            copy.start()

    squares = [jnp.zeros((answer, 128), F32) for _ in range(count)]
    for k in range(steps):
        at = slice(k * depth, (k + 1) * depth)
        for copy in copies[k]:
            copy.wait()
        for r in range(count):
            x = rows[k, r].astype(F32)
            x2 = x * x
            for j in range(depth // 128):
                squares[r] = squares[r] + x2[:, j * 128 : (j + 1) * 128]
            scaled[k, r * answer : (r + 1) * answer] = (x * gain[:, at]).astype(BF)
        partial = jnp.dot(scaled[k], weights[at], preferred_element_type=F32)
        if k == 0:
            product[...] = partial
        elif k < steps - 1:
            product[...] += partial
        else:
            partial = product[...] + partial
            lane = lax.broadcasted_iota(jnp.int32, (answer, 128), 1)
            for r in range(count):
                total = jnp.sum(squares[r], axis=-1, keepdims=True)
                high = total.astype(BF).astype(F32)
                pair = jnp.where(lane == 0, high, jnp.where(lane == 1, total - high, 0.0))
                for h in range(HALVES):
                    out = outs[r * HALVES + h]
                    start = r * answer + h * span
                    out[:, : queries + 2 * HD] = partial[start : start + span].astype(BF)
                    out[:, queries + 2 * HD :] = pair[h * span : (h + 1) * span].astype(BF)


def project(place, hidden, gain, w_query, w_key, w_value):
    count, answer, width = hidden.shape
    total = w_query.shape[1] + 2 * HD
    steps = 4
    smem = pl.BlockSpec(memory_space=pltpu.SMEM)
    vmem = pl.BlockSpec(memory_space=pltpu.VMEM)
    anywhere = pl.BlockSpec(memory_space=pl.ANY)
    return pl.pallas_call(
        project_kernel,
        in_specs=[smem, anywhere, vmem, anywhere, anywhere, anywhere],
        out_specs=[vmem] * (count * HALVES),
        out_shape=[jax.ShapeDtypeStruct((answer // HALVES, total + HD), BF)] * (count * HALVES),
        scratch_shapes=[
            pltpu.VMEM((steps, count, answer, width // steps), BF),
            pltpu.VMEM((width, total), BF),
            pltpu.VMEM((steps, count * answer, width // steps), BF),
            pltpu.VMEM((count * answer, total), F32),
            pltpu.SemaphoreType.DMA((steps, count + 3)),
        ],
        compiler_params=pltpu.CompilerParams(vmem_limit_bytes=60 * MIB),
        cost_estimate=pl.CostEstimate(
            flops=2 * count * answer * width * total, bytes_accessed=9 * MIB, transcendentals=0
        ),
        name="project",
    )(place, hidden, gain, w_query, w_key, w_value)


def attention_kernel(half, place, mask, p0, p1, p2, p3, cosine, sine, *rest):
    before, rest = (rest[:2], rest[2:]) if half else ((), rest)
    own_key, own_value, a1, b1, a3, b3, key2, value2, key2b, value2b, out, *rest = rest
    after, rest = ([], rest) if half == HALVES - 1 else (rest[:2], rest[2:])
    queries, near_key, near_value, keys, values, buf0, buf1, sem = rest
    section, core = place[0], place[1]
    span = p0.shape[0]
    answer = near_key.shape[0]
    heads = out.shape[1] // HD
    rows = heads * span
    local = own_key.shape[0]
    piece_rows = local // 2
    sections = keys.shape[0] // local

    copies = []

    def bring(source, buffer, start, size):
        copy = pltpu.make_async_copy(
            source,
            buffer.at[pl.ds(pl.multiple_of(start, size), size), pl.ds(0, HD)],
            sem.at[len(copies)],
        )
        copy.start()
        copies.append(copy)

    bring(own_key, keys, section * local, local)
    bring(own_value, values, section * local, local)
    pairs = [(r, p.at[0], p.at[1]) for r, p in ((1, a1), (1, b1), (3, a3), (3, b3))]
    pairs += [(2, key2, value2), (2, key2b, value2b)]
    for n, (r, *pair) in enumerate(pairs):
        source = lax.rem(section + sections - r, sections)
        side = core if n % 2 == 0 else 1 - core
        for piece, buffer in zip(pair, (keys, values)):
            bring(piece, buffer, source * local + side * piece_rows, piece_rows)

    first = jnp.where(lax.broadcasted_iota(jnp.int32, (rows, HD), 1) == 0, 1.0, 0.0).astype(BF)

    def fill(b, carry):
        at = pl.ds(pl.multiple_of(b * BLOCK, BLOCK), BLOCK)
        bias = jnp.where(mask[section, b] > 0, 0.0, masked_score)
        keys[at, HD:] = jnp.full((BLOCK, HD), bias, F32).astype(BF)
        values[at, HD:] = first[:BLOCK]
        return carry

    lax.fori_loop(0, keys.shape[0] // BLOCK, fill, 0, unroll=4)

    width = (heads + 2) * HD
    total = (
        p0[:, width:].astype(F32) + p1[:, width:].astype(F32)
        + p2[:, width:].astype(F32) + p3[:, width:].astype(F32)
    )
    scale = lax.rsqrt((total[:, 0:1] + total[:, 1:2]) / D + norm_eps)

    def column(h):
        at = slice(h * HD, (h + 1) * HD)
        return (
            p0[:, at].astype(F32) + p1[:, at].astype(F32)
            + p2[:, at].astype(F32) + p3[:, at].astype(F32)
        ) * scale

    def turned(x):
        return x * cosine[...] + pltpu.roll(x, HD // 2, 1) * sine[...]

    factor = math.log2(math.e) / math.sqrt(HD)
    for h in range(heads):
        queries[h * span : (h + 1) * span] = (turned(column(h)) * factor).astype(BF)
    new_key = turned(column(heads)).astype(BF)
    new_value = column(heads + 1).astype(BF)
    for ref, new in zip(after, (new_key, new_value)):
        ref[...] = new
    near_value[:, HD:] = first[:answer]
    for h in range(HALVES):
        at = slice(h * span, (h + 1) * span)
        if h == half:
            near_key[at], near_value[at, :HD] = new_key, new_value
        elif h < half:
            near_key[at], near_value[at, :HD] = before[0][...], before[1][...]
        else:
            near_key[at] = jnp.zeros((span, HD), BF)
            near_value[at, :HD] = jnp.zeros((span, HD), BF)

    tile = buf0.shape[1]
    tiles = keys.shape[0] // tile
    dims = (((1,), (1,)), ((), ()))
    q = queries[...]
    q_aug = jnp.concatenate([q, first], axis=1)
    s = lax.dot_general(q, near_key[...], dims, preferred_element_type=F32)
    row = lax.rem(lax.broadcasted_iota(jnp.int32, (rows, answer), 0), span) + half * span
    s = jnp.where(row >= lax.broadcasted_iota(jnp.int32, (rows, answer), 1), s, masked_score)
    m = jnp.max(s, axis=-1, keepdims=True)
    acc = jnp.dot(jnp.exp2(s - m).astype(BF), near_value[...], preferred_element_type=F32)

    for copy in copies:
        copy.wait()

    buffers = (buf0, buf1)
    each = tiles // LOOPS

    def at(t):
        return pl.ds(pl.multiple_of(t * tile, tile), tile)

    def sweep(i, state):
        m, acc = state

        def score(t):
            s = lax.dot_general(
                q_aug, keys[at(i * each + t)], dims, preferred_element_type=F32
            )
            buffers[t % 2][...] = s
            return jnp.max(s, axis=-1, keepdims=True)

        top = score(0)
        for t in range(each):
            m_new = jnp.maximum(m, top)
            if t + 1 < each:
                top = score(t + 1)
            p = jnp.exp2(buffers[t % 2][...] - m_new).astype(BF)
            acc = acc * jnp.exp2(m - m_new) + jnp.dot(
                p, values[at(i * each + t)], preferred_element_type=F32
            )
            m = m_new
        return m, acc

    m, acc = lax.fori_loop(0, LOOPS, sweep, (m, acc))
    result = (acc[:, :HD] / acc[:, HD : HD + 1]).astype(BF)
    for h in range(heads):
        out[:, h * HD : (h + 1) * HD] = result[h * span : (h + 1) * span]


def attend(half, place, mask, parts, cosine, sine, before, own_key, own_value, pieces):
    span = parts[0].shape[0]
    answer = span * HALVES
    context = NBLK * BLOCK
    heads = parts[0].shape[1] // HD - 3
    rows = heads * span
    vmem = pl.BlockSpec(memory_space=pltpu.VMEM)
    smem = pl.BlockSpec(memory_space=pltpu.SMEM)
    anywhere = pl.BlockSpec(memory_space=pl.ANY)
    extra = 0 if half == HALVES - 1 else 2
    outs = [jax.ShapeDtypeStruct((span, heads * HD), BF)]
    outs += [jax.ShapeDtypeStruct((span, HD), BF)] * extra
    return pl.pallas_call(
        functools.partial(attention_kernel, half),
        in_specs=[smem, smem] + [vmem] * (6 + len(before)) + [anywhere] * 10,
        out_specs=[vmem] * (1 + extra),
        out_shape=outs,
        scratch_shapes=[
            pltpu.VMEM((rows, HD), BF),
            pltpu.VMEM((answer, HD), BF),
            pltpu.VMEM((answer, 2 * HD), BF),
            pltpu.VMEM((context, 2 * HD), BF),
            pltpu.VMEM((context, 2 * HD), BF),
            pltpu.VMEM((rows, TILE), F32),
            pltpu.VMEM((rows, TILE), F32),
            pltpu.SemaphoreType.DMA((14,)),
        ],
        compiler_params=pltpu.CompilerParams(vmem_limit_bytes=32 * MIB),
        cost_estimate=pl.CostEstimate(
            flops=8 * rows * context * HD,
            bytes_accessed=6 * MIB,
            transcendentals=rows * context,
        ),
        name="attend",
    )(place, mask, *parts, cosine, sine, *before, own_key, own_value, *pieces)


def output_kernel(place, a0, a1, a2, a3, w_out, before, o0, o1, o2, o3, after, rows, weights, sem):
    count, span, depth = rows.shape
    outs = (o0, o1, o2, o3)
    after[...] = jnp.zeros_like(after)
    width = w_out.shape[1] // len(outs)
    copies = []
    for k in range(len(outs)):
        at = pl.ds(pl.multiple_of(lax.rem(place[2] + k, len(outs)) * width, width), width)
        copies.append(pltpu.make_async_copy(w_out.at[:, at], weights.at[k], sem.at[k]))
        copies[-1].start()
    for r, part in enumerate((a0, a1, a2, a3)):
        rows[lax.rem(place[0] + count - r, count)] = part[...]
    left = rows[...].reshape(count * span, depth)
    for k, out in enumerate(outs):
        copies[k].wait()
        for side in range(2):
            at = slice(side * width // 2, (side + 1) * width // 2)
            out[side] = jnp.dot(left, weights[k, :, at], preferred_element_type=F32).astype(
                out.dtype
            )


def project_out(place, parts, w_out, before):
    span, depth = parts[0].shape
    count = len(parts)
    width = w_out.shape[1] // 4
    vmem = pl.BlockSpec(memory_space=pltpu.VMEM)
    smem = pl.BlockSpec(memory_space=pltpu.SMEM)
    shape = (2, count * span, width // 2)
    return pl.pallas_call(
        output_kernel,
        in_specs=[smem] + [vmem] * count + [pl.BlockSpec(memory_space=pl.ANY)] * 2,
        out_specs=[vmem] * 5,
        out_shape=[jax.ShapeDtypeStruct(shape, F32)]
        + [jax.ShapeDtypeStruct(shape, BF)] * 3
        + [jax.ShapeDtypeStruct((8, 128), F32)],
        scratch_shapes=[
            pltpu.VMEM((count, span, depth), BF),
            pltpu.VMEM((4, depth, width), BF),
            pltpu.SemaphoreType.DMA((4,)),
        ],
        compiler_params=pltpu.CompilerParams(vmem_limit_bytes=24 * MIB),
        cost_estimate=pl.CostEstimate(
            flops=8 * count * span * depth * width, bytes_accessed=6 * MIB, transcendentals=0
        ),
        name="project_out",
    )(place, *parts, w_out, before)


def reduce_kernel(place, before, *refs):
    pieces, (send, keep) = refs[:-2], refs[-2:]
    for side, out in ((1 - place[3], send), (place[3], keep)):
        total = pieces[0][side].astype(F32)
        for piece in pieces[1:]:
            total = total + piece[side].astype(F32)
        out[...] = total.astype(out.dtype)


def reduce_pieces(place, before, pieces):
    _, rows, width = pieces[0].shape
    vmem = pl.BlockSpec(memory_space=pltpu.VMEM)
    return pl.pallas_call(
        reduce_kernel,
        in_specs=[pl.BlockSpec(memory_space=pltpu.SMEM), pl.BlockSpec(memory_space=pl.ANY)]
        + [vmem] * len(pieces),
        out_specs=[vmem] * 2,
        out_shape=[jax.ShapeDtypeStruct((rows, width), t) for t in (BF, F32)],
        compiler_params=pltpu.CompilerParams(vmem_limit_bytes=16 * MIB),
        cost_estimate=pl.CostEstimate(flops=8 * rows * width, bytes_accessed=16 * rows * width, transcendentals=0),
        name="reduce_pieces",
    )(place, before, *pieces)


def finish_kernel(earlier, keep, arrived, out):
    count, rows, _ = out.shape
    start = earlier.shape[1]
    out[:, :start] = earlier[...]
    total = (keep[...] + arrived[...].astype(F32)).astype(out.dtype)
    for c in range(count):
        out[c, start:] = total[c * (rows - start) : (c + 1) * (rows - start)]


def finish(earlier, keep, arrived):
    count, rows, width = earlier.shape
    vmem = pl.BlockSpec(memory_space=pltpu.VMEM)
    return pl.pallas_call(
        finish_kernel,
        in_specs=[vmem] * 3,
        out_specs=vmem,
        out_shape=jax.ShapeDtypeStruct((count, rows + keep.shape[0] // count, width), BF),
        compiler_params=pltpu.CompilerParams(vmem_limit_bytes=16 * MIB),
        name="finish",
    )(earlier, keep, arrived)


def rotation(answer):
    half = HD // 2
    positions = (NBLK * BLOCK + jnp.arange(answer)).astype(F32)
    frequency = rope_base ** (-2.0 * jnp.arange(half).astype(F32) / HD)
    angles = positions[:, None] * frequency[None, :]
    cosine, sine = jnp.cos(angles), jnp.sin(angles)
    return jnp.concatenate([cosine, cosine], axis=1), jnp.concatenate([-sine, sine], axis=1)


def per_device(
    hidden, norm_gain, w_query, w_key, w_value, w_out, cache_key, cache_value, block_mask
):
    section = lax.axis_index("section")
    core = lax.rem(lax.axis_index("coal"), 2)
    tensor = lax.axis_index("tensor")
    z_hi = lax.rem(tensor, 2)
    place = jnp.stack([section, core, tensor // 2, z_hi]).astype(jnp.int32)
    answer = hidden.shape[1]
    span = answer // HALVES
    half_rows = cache_key.shape[0] // 2
    piece = jnp.stack(
        [
            lax.dynamic_slice_in_dim(cache_key, core * half_rows, half_rows, 0),
            lax.dynamic_slice_in_dim(cache_value, core * half_rows, half_rows, 0),
        ]
    )
    with jax.named_scope("cache"):
        mine1, mine3 = section_shift(piece, 1), section_shift(piece, 3)
    with jax.named_scope("forward"):
        key2, value2 = section_shift(mine1[0], 1), section_shift(mine3[1], 3)
    with jax.named_scope("swap"):
        pieces = (mine1, core_swap(mine1), mine3, core_swap(mine3))
        pieces += (key2, value2, core_swap(key2), core_swap(value2))
    cosine, sine = rotation(answer)

    chunks = project(place, hidden, norm_gain[None, :], w_query, w_key, w_value)
    parts = []
    for h in range(HALVES):
        with jax.named_scope(f"sums{h}"):
            parts.append(
                [chunks[h]] + [section_shift(chunks[r * HALVES + h], r) for r in (2, 3, 1)]
            )
    before, attended, gathered = [], [], []
    for h in range(HALVES):
        at = slice(h * span, (h + 1) * span)
        attention, *before = attend(
            h, place, block_mask, parts[h], cosine[at], sine[at], before,
            cache_key, cache_value, pieces,
        )
        attended.append(attention)
        with jax.named_scope(f"gather{h}"):
            gathered.append([attention] + [section_shift(attention, r) for r in (1, 2, 3)])

    turn, send = attended[-1], attended[0]
    for h in range(HALVES):
        *sums, turn = project_out(place, gathered[h], w_out, turn)
        with jax.named_scope(f"x{h}"):
            pieces = [sums[0]] + [x_shift(sums[r], r) for r in (2, 3, 1)]
        send, keep = reduce_pieces(place, send, pieces)
        with jax.named_scope(f"z{h}"):
            arrived = z_swap(send)
        if h == 0:
            result = (keep + arrived.astype(F32)).astype(BF)
            result = result.reshape(hidden.shape[0], answer // HALVES, -1)
        else:
            result = finish(result, keep, arrived)
    return result


def solution(mesh):
    return jax.shard_map(
        per_device,
        mesh=mesh,
        in_specs=(
            P("coal", None, "section"),
            P("section"),
            P("section", "tensor"),
            P("section", "tensor"),
            P("section", "tensor"),
            P("tensor", "section"),
            P("section", "tensor"),
            P("section", "tensor"),
            P("coal", None),
        ),
        out_specs=P("coal", None, ("section", "tensor")),
        check_vma=False,
    )
```
